128 devices in a mesh: row: 8 (over x, z_lo), col: 16 (over y, z_hi, core).
Axes of the slice: x: 4, y: 4, z: 4 (z_hi: 2, z_lo: 2; z = z_hi * 2 + z_lo), core: 2. Of those that a mesh axis runs over, the one named last changes fastest.
Arguments:
- family_embedding: bfloat16 [128, 1024, 256], P('col', 'row'), may hold values from -6 to 6
- pairwise_embedding: bfloat16 [1024, 1024, 128], P('row', 'col'), may hold values from -6 to 6
- family_presence: int32 [128, 1024], P('col', 'row'), may hold values 0 or 1
- amino_validity: int32 [1024], replicated, may hold values from 0 to 1, as said below
- horizontal_query_projector: bfloat16 [4, 256, 256], replicated
- horizontal_final_projector: bfloat16 [256, 256], replicated, may hold values from -0.375 to 0.375
- pairwise_offset_factor: bfloat16 [128, 8], replicated, may hold values from -0.5 to 0.5
- vertical_query_projector: bfloat16 [4, 256, 256], replicated
- vertical_final_projector: bfloat16 [256, 256], replicated, may hold values from -0.375 to 0.375
- tensor_sided_projector: bfloat16 [2, 256, 32], replicated, may hold values from -0.375 to 0.375
- tensor_final_projector: bfloat16 [1024, 128], replicated, may hold values from -0.75 to 0.75
Outputs:
- alignment_output: bfloat16 [128, 1024, 256], P('col', 'row')
- pair_increment: bfloat16 [1024, 1024, 128], P('row', 'col')
The draws below stay inside these ranges and needn't reach their ends.
Inputs may be any that keep to these rules, and one draw needn't show every extreme that they name: `amino_validity`: residues come in consecutive blocks of 64; each block ends with a padded tail of 0 to 32 zeros, and before that tail a residue may also be 0 (unresolved).
All inputs are finite; a program needn't handle non-finite values. No bound on the sum of `family_presence` on one device may be relied on, other than what follows from the above.
Results may differ from the reference program's by a relative error of at most 0.019.
Values may be sent and summed in bfloat16 or wider, within the bound.
A program may use at most 128 MiB of HBM per device.

```python
import math
import jax
import jax.numpy as jnp
from jax import lax

FEATURE_DIM = 256
CZ = 128
HEAD_NUMBER = 8
HEAD_DIM = 32
HIDDEN_WIDTH = 32
RES_COL = 64
HOMOLOG_NUMBER = 128
CHAIN_LENGTH = 1024
N_ROW = 8


def attention_weights(key, stretch):
    parallel_flows = jax.random.split(key, 2)
    starting_parameters = jax.random.normal(parallel_flows[0], (4, FEATURE_DIM, HEAD_NUMBER * HEAD_DIM), jnp.float32) * FEATURE_DIM ** (-0.5)
    head_scale = jnp.exp(jax.random.uniform(parallel_flows[1], (HEAD_NUMBER,), jnp.float32, 0.0, math.log(stretch)))
    column_scale = jnp.repeat(head_scale, HEAD_DIM)
    query_weight = starting_parameters[0] * column_scale
    key_weight = starting_parameters[1] * column_scale
    return jnp.stack([query_weight, key_weight, starting_parameters[2], starting_parameters[3]])


def draw_horizontal_query_projector(key, part):
    key = jax.random.fold_in(key, 21)
    return attention_weights(key, 1.0).astype(jnp.bfloat16)


def draw_vertical_query_projector(key, part):
    key = jax.random.fold_in(key, 37)
    return attention_weights(key, 1.0).astype(jnp.bfloat16)


def draw_amino_validity(key, part):
    key = jax.random.fold_in(key, 5)
    parallel_flows = jax.random.split(key, 2)
    block_count = CHAIN_LENGTH // RES_COL
    tails = jax.random.randint(parallel_flows[0], (block_count, 1), 0, RES_COL // 2 + 1)
    places = jnp.arange(RES_COL, dtype=jnp.int32)[None, :]
    kept = (places < RES_COL - tails).astype(jnp.int32)
    resolved = (jax.random.randint(parallel_flows[1], (block_count, RES_COL), 0, 16) != 0).astype(jnp.int32)
    return (kept * resolved).reshape(CHAIN_LENGTH)


def touch_ends(drawn, key, least, largest):
    dims = drawn.shape
    spot = [jax.random.randint(jax.random.fold_in(key, axis), (), 0, dims[axis]) for axis in range(len(dims))]
    drawn = drawn.at[tuple(spot)].set(least)
    longest = dims.index(max(dims))
    spot[longest] = (spot[longest] + 1) % dims[longest]
    return drawn.at[tuple(spot)].set(largest)


def level_of(own_key, dims, cuts, smallest, high):
    def one(position, parts):
        heights = jax.random.uniform(jax.random.fold_in(jax.random.fold_in(own_key, 6), position), (parts,), jnp.float32, smallest / len(cuts), high / len(cuts))
        return jnp.repeat(jnp.exp(heights), dims[position] // parts).reshape((-1,) + (1,) * (len(dims) - position - 1))

    level = one(*cuts[0])
    for cut in cuts[1:]:
        level = level * one(*cut)
    return level


def noise(rng, extent, deviation, most, cuts=(), kind=jnp.bfloat16):
    level = level_of(rng, extent, cuts, -0.22, 0.18) if cuts else 1.0
    result = jax.random.normal(rng, extent, jnp.float32) * deviation * level
    return jnp.minimum(jnp.maximum(result, -most), most).astype(kind)


def setup_inputs(seed: int = 0) -> dict:
    keys = jax.random.split(jax.random.key(seed), 12)
    family_embedding = noise(keys[0], (HOMOLOG_NUMBER, CHAIN_LENGTH, FEATURE_DIM), 1.0, 6.0, ((0, 16), (1, 8)))
    pairwise_embedding = noise(keys[1], (CHAIN_LENGTH, CHAIN_LENGTH, CZ), 1.0, 6.0, ((0, 8), (1, 16)))
    family_presence = touch_ends((jax.random.randint(keys[2], (HOMOLOG_NUMBER, CHAIN_LENGTH), 0, 8) < 7).astype(jnp.int32), jax.random.fold_in(keys[2], 1), 0, 1)
    amino_validity = draw_amino_validity(jax.random.fold_in(keys[11], 71), 0)
    horizontal_query_projector = draw_horizontal_query_projector(jax.random.fold_in(keys[11], 71), 0)
    horizontal_final_projector = noise(keys[5], (HEAD_NUMBER * HEAD_DIM, FEATURE_DIM), (HEAD_NUMBER * HEAD_DIM) ** -0.5, 0.375)
    pairwise_offset_factor = noise(keys[6], (CZ, HEAD_NUMBER), CZ ** -0.5, 0.5)
    vertical_query_projector = draw_vertical_query_projector(jax.random.fold_in(keys[11], 71), 0)
    vertical_final_projector = noise(keys[8], (HEAD_NUMBER * HEAD_DIM, FEATURE_DIM), (HEAD_NUMBER * HEAD_DIM) ** -0.5, 0.375)
    tensor_sided_projector = noise(keys[9], (2, FEATURE_DIM, HIDDEN_WIDTH), FEATURE_DIM ** -0.5, 0.375)
    tensor_final_projector = noise(keys[10], (HIDDEN_WIDTH * HIDDEN_WIDTH, CZ), (HIDDEN_WIDTH * HIDDEN_WIDTH // 16) ** -0.5, 0.75)
    return dict(family_embedding=family_embedding, pairwise_embedding=pairwise_embedding, family_presence=family_presence, amino_validity=amino_validity, horizontal_query_projector=horizontal_query_projector, horizontal_final_projector=horizontal_final_projector, pairwise_offset_factor=pairwise_offset_factor, vertical_query_projector=vertical_query_projector, vertical_final_projector=vertical_final_projector, tensor_sided_projector=tensor_sided_projector, tensor_final_projector=tensor_final_projector)


LAYER_EPS = 1e-05
MASK_BIG = 1000000000.0

def standardize_features(values_in):
    centred = values_in - lax.optimization_barrier(jnp.mean(values_in, axis=-1, keepdims=True))
    spread = lax.optimization_barrier(jnp.mean(centred * centred, axis=-1, keepdims=True))
    return centred * lax.rsqrt(spread + LAYER_EPS)

def affine_mapping(standardized_source, weight):
    return jnp.dot(standardized_source, weight, preferred_element_type=jnp.float32)

def softmax_rows(scores):
    highest = lax.optimization_barrier(jnp.max(scores, axis=-1, keepdims=True))
    raised = jnp.exp(scores - highest)
    return raised / lax.optimization_barrier(jnp.sum(raised, axis=-1, keepdims=True))

def reference(family_embedding, pairwise_embedding, family_presence, amino_validity, horizontal_query_projector, horizontal_final_projector, pairwise_offset_factor, vertical_query_projector, vertical_final_projector, tensor_sided_projector, tensor_final_projector):
    present_mask = (family_presence * amino_validity[None, :]).astype(jnp.float32)
    inv_root = HEAD_DIM ** (-0.5)
    standardized_source = standardize_features(family_embedding.astype(jnp.float32)).astype(jnp.bfloat16)
    query_rows = (affine_mapping(standardized_source, horizontal_query_projector[0]) * inv_root).astype(jnp.bfloat16)
    key_rows = affine_mapping(standardized_source, horizontal_query_projector[1]).astype(jnp.bfloat16)
    value_rows = affine_mapping(standardized_source, horizontal_query_projector[2]).astype(jnp.bfloat16)
    horizontal_sigmoid_factor = jax.nn.sigmoid(affine_mapping(standardized_source, horizontal_query_projector[3]))
    pair_normed = standardize_features(pairwise_embedding.astype(jnp.float32)).astype(jnp.bfloat16)
    bias_heads = affine_mapping(pair_normed, pairwise_offset_factor).astype(jnp.bfloat16).transpose(2, 0, 1).astype(jnp.float32)

    def row_one(pieces):
        query_one, key_one, value_one, mask_one = pieces
        scores = jnp.einsum('ihd,jhd->hij', query_one.astype(jnp.float32).reshape(CHAIN_LENGTH, HEAD_NUMBER, HEAD_DIM), key_one.astype(jnp.float32).reshape(CHAIN_LENGTH, HEAD_NUMBER, HEAD_DIM))
        scores = jnp.where(mask_one[None, None, :] > 0.5, scores + bias_heads, -MASK_BIG)
        weights = softmax_rows(scores).astype(jnp.bfloat16)
        attended = jnp.einsum('hij,jhd->ihd', weights.astype(jnp.float32), value_one.astype(jnp.float32).reshape(CHAIN_LENGTH, HEAD_NUMBER, HEAD_DIM))
        return attended.reshape(CHAIN_LENGTH, HEAD_NUMBER * HEAD_DIM)
    horizontal_softmax_update = lax.map(row_one, (query_rows, key_rows, value_rows, present_mask))
    interim_family = (family_embedding.astype(jnp.float32) + affine_mapping((horizontal_sigmoid_factor * horizontal_softmax_update).astype(jnp.bfloat16), horizontal_final_projector)).astype(jnp.bfloat16)
    normalized_between = standardize_features(interim_family.astype(jnp.float32)).astype(jnp.bfloat16)
    query_cols = (affine_mapping(normalized_between, vertical_query_projector[0]) * inv_root).astype(jnp.bfloat16)
    key_cols = affine_mapping(normalized_between, vertical_query_projector[1]).astype(jnp.bfloat16)
    value_cols = affine_mapping(normalized_between, vertical_query_projector[2]).astype(jnp.bfloat16)
    column_gate = jax.nn.sigmoid(affine_mapping(normalized_between, vertical_query_projector[3]))
    block_count = CHAIN_LENGTH // RES_COL

    def to_blocks(arranged):
        return arranged.transpose(1, 0, 2).reshape(block_count, RES_COL, HOMOLOG_NUMBER, HEAD_NUMBER * HEAD_DIM)
    mask_blocks = present_mask.T.reshape(block_count, RES_COL, HOMOLOG_NUMBER)

    def col_block(pieces):
        query_one, key_one, value_one, mask_one = pieces
        scores = jnp.einsum('bshd,bthd->bhst', query_one.astype(jnp.float32).reshape(RES_COL, HOMOLOG_NUMBER, HEAD_NUMBER, HEAD_DIM), key_one.astype(jnp.float32).reshape(RES_COL, HOMOLOG_NUMBER, HEAD_NUMBER, HEAD_DIM))
        scores = jnp.where(mask_one[:, None, None, :] > 0.5, scores, -MASK_BIG)
        weights = softmax_rows(scores).astype(jnp.bfloat16)
        attended = jnp.einsum('bhst,bthd->bshd', weights.astype(jnp.float32), value_one.astype(jnp.float32).reshape(RES_COL, HOMOLOG_NUMBER, HEAD_NUMBER, HEAD_DIM))
        return attended.reshape(RES_COL, HOMOLOG_NUMBER, HEAD_NUMBER * HEAD_DIM)
    column_attended = lax.map(col_block, (to_blocks(query_cols), to_blocks(key_cols), to_blocks(value_cols), mask_blocks))
    column_attended = column_attended.reshape(CHAIN_LENGTH, HOMOLOG_NUMBER, HEAD_NUMBER * HEAD_DIM).transpose(1, 0, 2)
    alignment_output = (interim_family.astype(jnp.float32) + affine_mapping((column_gate * column_attended).astype(jnp.bfloat16), vertical_final_projector)).astype(jnp.bfloat16)
    normalized_output = standardize_features(alignment_output.astype(jnp.float32)).astype(jnp.bfloat16)
    left = (affine_mapping(normalized_output, tensor_sided_projector[0]) * present_mask[:, :, None]).astype(jnp.bfloat16)
    right = (affine_mapping(normalized_output, tensor_sided_projector[1]) * present_mask[:, :, None]).astype(jnp.bfloat16)
    pair_count = jnp.dot(present_mask.T, present_mask, precision=lax.Precision.HIGHEST)
    row_block = N_ROW
    left_blocks = left.reshape(HOMOLOG_NUMBER, CHAIN_LENGTH // row_block, row_block, HIDDEN_WIDTH).transpose(1, 0, 2, 3)
    right_float = right.astype(jnp.float32)

    def opm_block(left_one):
        outer = jnp.einsum('sic,sjd->ijcd', left_one.astype(jnp.float32), right_float)
        outer = outer.astype(jnp.bfloat16).reshape(row_block, CHAIN_LENGTH, HIDDEN_WIDTH * HIDDEN_WIDTH)
        return affine_mapping(outer, tensor_final_projector)
    summed = lax.map(opm_block, left_blocks).reshape(CHAIN_LENGTH, CHAIN_LENGTH, CZ)
    pair_increment = (summed / jnp.maximum(pair_count, 1.0)[:, :, None]).astype(jnp.bfloat16)
    return (alignment_output, pair_increment)
```

```python
import jax
import jax.numpy as jnp
from jax import lax
from jax.experimental import pallas as pl
from jax.experimental.pallas import tpu as pltpu
from jax.sharding import PartitionSpec as P

BF = jnp.bfloat16
F32 = jnp.float32
EPS = 1e-05
MASK_BIG = 1000000000.0
MESH = pl.DeviceIdType.MESH

NR = 8
NC = 16
S = 8
R = 128
D = 256
H = 8
HD = 32
G = 4
HP = 2


def norm(x):
    c = x - jnp.mean(x, axis=-1, keepdims=True)
    return c * lax.rsqrt(jnp.mean(c * c, axis=-1, keepdims=True) + EPS)


def dot(a, b):
    return jnp.dot(a, b, preferred_element_type=F32)


def dot_t(a, b):
    return lax.dot_general(a, b, (((1,), (1,)), ((), ())), preferred_element_type=F32)


def sigmoid(x):
    return 1.0 / (1.0 + jnp.exp(-x))


def head_lanes(rows):
    return lax.broadcasted_iota(jnp.int32, (rows, D), 1) // HD


def attend(q, k, v, score_of):
    n = q.shape[0]
    lanes = head_lanes(n)
    total = jnp.zeros((n, D), F32)
    for h0 in range(0, H, HP):
        heads = range(h0, h0 + HP)
        stacked = jnp.concatenate([jnp.where(lanes == h, q, jnp.zeros_like(q)) for h in heads], axis=0)
        raw = dot_t(stacked, k)
        parts, sums = [], []
        for at, h in enumerate(heads):
            s = score_of(h, raw[at * n:(at + 1) * n])
            p = jnp.exp(s - jnp.max(s, axis=-1, keepdims=True))
            sums.append(jnp.sum(p, axis=-1, keepdims=True))
            parts.append(p.astype(BF))
        out = dot(jnp.concatenate(parts, axis=0), v)
        for at, h in enumerate(heads):
            total = jnp.where(lanes == h, out[at * n:(at + 1) * n] * (1.0 / sums[at]), total)
    return total


def msa_kernel(
    fam, pair, present, valid, wh, wo, wb, wv, wvo, wlr,
    align, lt_out, rt_out, inv_out,
    nall, live, bscr, mine, sib, ball, qs, gs, ks, vs, midf, snd, rcv,
    xf, nf, upf, back_snd, back_rcv, lf, rf, lsnd, lrcv, rsnd, rrcv, ltt, cmask,
    n_s, n_r, lv_s, lv_r, lc_s, lc_r, sb_s, sb_r, b_s, b_r, bc_s, bc_r,
    m_s, m_r, u_s, u_r, le_s, le_r, ri_s, ri_r,
):
    r = lax.axis_index("row")
    c = lax.axis_index("col")
    core = lax.rem(c, 2)
    blk = c // 2

    def flip(i):
        return i + 1 - 2 * lax.rem(i, 2)

    def copy(src, dst, ss, rs, row, col):
        return pltpu.make_async_remote_copy(
            src_ref=src, dst_ref=dst, send_sem=ss, recv_sem=rs, device_id=(row, col), device_id_type=MESH
        )

    rz, rl, rr, rf2 = flip(r), lax.rem(r + 6, 8), lax.rem(r + 2, 8), lax.rem(r + 4, 8)

    def ncopy(g, slot, block, lo, n, to):
        ref = nall.at[block, pl.ds(2 * g + lo, n)]
        return copy(ref, ref, n_s.at[g, slot], n_r.at[g, slot], to, c)

    n_plan = [
        (r, 0, 2, rz), (r, 0, 2, rr), (r, 0, 2, rl), (rz, 0, 2, rr), (rz, 0, 2, rl),
        (rl, 0, 1, rr), (rr, 1, 1, rl), (rf2, 0, 2, rz),
    ]

    def n_slot(g, i):
        return ncopy(g, i, *n_plan[i])

    def n1(g):
        for i in (0, 1, 2):
            n_slot(g, i).start()

    def n2(g):
        for i in (0, 1, 2):
            n_slot(g, i).wait_recv()
        for i in (3, 4, 5, 6):
            n_slot(g, i).start()

    def n3(g):
        for i in (5, 6):
            n_slot(g, i).wait_recv()
        n_slot(g, 7).start()

    def n4(g):
        for i in (3, 4, 7):
            n_slot(g, i).wait_recv()

    h0 = core * 4
    cz, cl, cr, cs = c + 2 - 4 * lax.rem(blk, 2), lax.rem(c + 12, 16), lax.rem(c + 4, 16), flip(c)
    bz, bl, br, bf2 = flip(blk), lax.rem(blk + 6, 8), lax.rem(blk + 2, 8), lax.rem(blk + 4, 8)

    def bcopy(slot, block, lo, n, to):
        ref = ball.at[block, pl.ds(h0 + lo, n)]
        return copy(ref, ref, b_s.at[slot], b_r.at[slot], r, to)

    b_slots = [
        bcopy(0, blk, 0, 4, cz), bcopy(1, blk, 0, 4, cr), bcopy(2, blk, 0, 4, cl),
        bcopy(3, bz, 0, 4, cr), bcopy(4, bz, 0, 4, cl),
        bcopy(5, bl, 0, 2, cr), bcopy(6, br, 2, 2, cl), bcopy(7, bf2, 0, 4, cz),
    ]

    def bcore(slot, block):
        ref = ball.at[block, pl.ds(h0, 4)]
        return copy(ref, ref, bc_s.at[slot], bc_r.at[slot], r, cs)

    bc_slots = [
        bcore(0, bz), bcore(1, bl), bcore(2, br), bcore(3, flip(bl)), bcore(4, flip(br)),
        bcore(5, bf2), bcore(6, flip(bf2)),
    ]

    for s in range(S):
        nall[r, s] = norm(fam[s].astype(F32)).astype(BF)
    live[c, r] = (present[...] * valid[pl.ds(r, 1), :]).astype(F32)
    n1(0)
    n1(1)

    def lv(k):
        ref = live.at[c, r]
        return copy(ref, ref, lv_s.at[k], lv_r.at[k], lax.rem(r + k, 8), c)

    for k in range(1, 8):
        lv(k).start()

    def bias_step(t, carry):
        lo = pair[pl.ds(t * 8, 8)].astype(F32)
        hi = pair[pl.ds(64 + t * 8, 8)].astype(F32)
        x = norm(jnp.concatenate([lo, hi], axis=1).reshape(1024, 128)).astype(BF)
        b = dot_t(wb[...], x)
        for i in range(8):
            bscr[pl.ds(t * 64 + i * 8, 8), :] = b[:, i * 128:(i + 1) * 128]
        return carry

    lax.fori_loop(0, 8, bias_step, 0)
    for h in range(H):
        mine[h] = bscr[pl.ds(h, 64, stride=8), :].astype(BF)
    sib_copy = copy(mine, sib, sb_s, sb_r, r, cs)
    sib_copy.start()
    n2(0)
    n1(2)

    def qg_step(s, carry):
        x = nall[r, s]
        qs[s] = (dot(x, wh[0]) * (HD ** -0.5)).astype(BF)
        gs[s] = sigmoid(dot(x, wh[3]))
        return carry

    lax.fori_loop(0, S, qg_step, 0)

    sib_copy.wait_recv()
    low = lax.broadcasted_iota(jnp.int32, (64, 128), 1) < 64
    for h in range(H):
        a = mine[h].astype(F32)
        b = sib[h].astype(F32)
        first = jnp.where(core == 0, a, b)
        second = jnp.where(core == 0, b, a)
        ball[blk, h, 0:64, :] = jnp.where(low, first, pltpu.roll(second, 64, 1)).astype(BF)
        ball[blk, h, 64:128, :] = jnp.where(low, pltpu.roll(first, 64, 1), second).astype(BF)
    for i in (0, 1, 2):
        b_slots[i].start()
    n2(1)
    n3(0)
    for k in range(1, 8):
        lv(k).wait_recv()

    def lc(k):
        ref = live.at[c]
        return copy(ref, ref, lc_s.at[k], lc_r.at[k], r, lax.rem(c + k, 16))

    for k in range(1, 16):
        lc(k).start()
    for i in (0, 1, 2):
        b_slots[i].wait_recv()
    for i in (3, 4, 5, 6):
        b_slots[i].start()
    for i in (0, 1, 2):
        bc_slots[i].start()
    for i in (5, 6):
        b_slots[i].wait_recv()
    b_slots[7].start()
    bc_slots[5].start()
    for i in (3, 4):
        b_slots[i].wait_recv()
    for i in (3, 4):
        bc_slots[i].start()
    b_slots[7].wait_recv()
    bc_slots[6].start()
    for i in range(7):
        bc_slots[i].wait_recv()

    def mcopy(g, k):
        to = lax.rem(c + k, 16)
        rows = pl.ds(g * 16, 16)
        return copy(snd.at[to, rows], rcv.at[c, rows], m_s.at[g, k], m_r.at[g, k], r, to)

    def group(g, carry):
        @pl.when(g < G - 3)
        def _():
            n1(g + 3)

        @pl.when(g < G - 2)
        def _():
            n2(g + 2)

        @pl.when(g < G - 1)
        def _():
            n3(g + 1)

        n4(g)

        def row_one(i, carry):
            s = 2 * g + i
            for b in range(NR):
                x = nall[b, s]
                ks[b * R:(b + 1) * R, :] = dot(x, wh[1]).astype(BF)
                vs[b * R:(b + 1) * R, :] = dot(x, wh[2]).astype(BF)
            keep = jnp.concatenate([live[c, b, pl.ds(s, 1), :] for b in range(NR)], axis=1) > 0.5

            def score(h, raw):
                bias = jnp.concatenate([ball[b, h] for b in range(NR)], axis=1)
                return jnp.where(keep, raw + bias.astype(F32), -MASK_BIG)

            o = attend(qs[s], ks[...], vs[...], score)
            gated = (gs[s] * o).astype(BF)
            midf[i] = fam[s].astype(F32) + dot(gated, wo[...])
            return carry

        lax.fori_loop(0, 2, row_one, 0)
        for t in range(NC):
            two = jnp.concatenate([midf[0, t * 8:(t + 1) * 8, :], midf[1, t * 8:(t + 1) * 8, :]], axis=0)
            snd[t, pl.ds(pl.multiple_of(g * 16, 16), 16), :] = two.astype(BF)
        for k in range(1, 16):
            mcopy(g, k).start()
        return carry

    lax.fori_loop(0, G, group, 0)
    rcv[c] = snd[c]
    for k in range(1, 16):
        lc(k).wait_recv()
    by_res = live[:, r].reshape(R, R).T
    cmask[...] = by_res
    by_col = live[:, blk].reshape(R, R).T
    ltt[...] = by_col
    right_live = ltt[pl.ds(pl.multiple_of(core * 64, 64), 64), :]
    inv_out[...] = 1.0 / jnp.maximum(dot_t(right_live.astype(BF), by_res.astype(BF)), 1.0)
    for g in range(G):
        for k in range(1, 16):
            mcopy(g, k).wait_recv()

    def col_norm(t, carry):
        x = rcv[t].astype(F32)
        rows = pl.ds(pl.multiple_of(t * 64, 64), 64)
        y = norm(x)
        for i in range(2):
            xf[i, rows, :] = x[:, i * 128:(i + 1) * 128]
            nf[i, rows, :] = y[:, i * 128:(i + 1) * 128]
        return carry

    lax.fori_loop(0, NC, col_norm, 0)

    def col_one(b, carry):
        every = pl.ds(b, R, stride=8)
        x = jnp.concatenate([nf[i, every, :] for i in range(2)], axis=1).astype(BF)
        q = (dot(x, wv[0]) * (HD ** -0.5)).astype(BF)
        k = dot(x, wv[1]).astype(BF)
        v = dot(x, wv[2]).astype(BF)
        gate = sigmoid(dot(x, wv[3]))
        row = cmask[pl.ds(c * 8 + b, 1), :]

        def score(h, raw):
            return jnp.where(row > 0.5, raw, -MASK_BIG)

        o = attend(q, k, v, score)
        up = jnp.concatenate([xf[i, every, :] for i in range(2)], axis=1) + dot((gate * o).astype(BF), wvo[...])
        up = up.astype(BF).astype(F32)
        for i in range(2):
            upf[i, every, :] = up[:, i * 128:(i + 1) * 128]
        both = dot_t(wlr[...], norm(up).astype(BF)) * row
        lf[pl.ds(b, HD, stride=8), :] = both[:HD]
        rf[pl.ds(pl.multiple_of(b * HD, HD), HD), :] = both[HD:]
        return carry

    lax.fori_loop(0, 8, col_one, 0)
    lsnd[...] = lf[...].astype(BF)
    rsnd[...] = rf[...].astype(BF)

    def lcopy(k):
        return copy(lsnd, lrcv.at[c], le_s.at[k], le_r.at[k], r, lax.rem(c + k, 16))

    for k in range(1, 16):
        lcopy(k).start()

    target = 2 * r + c // 8
    place = lax.rem(c, 8)
    self_row = jnp.where(target == c, r, -1)

    def rcopy(k, row):
        return copy(rsnd, rrcv.at[place], ri_s.at[k], ri_r.at[place], row, target)

    for k in range(8):
        @pl.when(self_row != k)
        def _():
            rcopy(k, k).start()

    @pl.when(target == c)
    def _():
        rrcv[place] = rsnd[...]

    for i in range(2):
        back_snd[:, :, i * 128:(i + 1) * 128] = upf[i].reshape(NC, 64, 128).astype(BF)

    def ucopy(k):
        to = lax.rem(c + k, 16)
        return copy(back_snd.at[to], back_rcv.at[c], u_s.at[k], u_r.at[k], r, to)

    for k in range(1, 16):
        ucopy(k).start()
    lrcv[c] = lsnd[...]
    back_rcv[c] = back_snd[c]

    for k in range(1, 16):
        lcopy(k).wait_recv()
    for i in range(HD):
        lt_out[i * R:(i + 1) * R, :] = jnp.concatenate(
            [lrcv[t, i * 8:(i + 1) * 8, :] for t in range(NC)], axis=0
        )

    source_row = blk
    for k in range(8):
        source_col = 8 * core + k

        @pl.when(jnp.logical_or(source_row != r, source_col != c))
        def _():
            copy(rsnd, rrcv.at[k], ri_s.at[k], ri_r.at[k], r, c).wait_recv()

    rt_out[...] = rrcv[...].reshape(8 * 256, 128)

    for k in range(1, 16):
        ucopy(k).wait_recv()
    for s in range(S):
        rows = [back_rcv[t, s * 8:(s + 1) * 8, :] for t in range(NC)]
        align[s] = jnp.concatenate(rows, axis=0)

    for g in range(G):
        for i in range(8):
            n_slot(g, i).wait_send()
        for k in range(1, 16):
            mcopy(g, k).wait_send()
    for k in range(1, 8):
        lv(k).wait_send()
    for k in range(1, 16):
        lc(k).wait_send()
        lcopy(k).wait_send()
        ucopy(k).wait_send()
    sib_copy.wait_send()
    for cp in b_slots + bc_slots:
        cp.wait_send()
    for k in range(8):
        @pl.when(self_row != k)
        def _():
            rcopy(k, k).wait_send()


def opm_kernel(lt, rt, inv, w, out, wt, acc):
    @pl.when(pl.program_id(0) == 0)
    def _():
        wt[...] = w[...].astype(F32).T.astype(BF)

    def step(t, carry):
        rows = rt[pl.ds(pl.multiple_of(t * 64, 64), 64), :]
        o = dot_t(rows, lt[...]).astype(BF)
        two = jnp.concatenate(
            [
                jnp.concatenate([o[j * HD:(j + 1) * HD, i * R:(i + 1) * R] for i in range(HD)], axis=0)
                for j in range(2)
            ],
            axis=1,
        )
        y = dot(wt[...], two)
        for j in range(2):
            one = y[:, j * R:(j + 1) * R] * inv[pl.ds(2 * t + j, 1), :]
            acc[pl.ds(2 * t + j, R, stride=16), :] = one.T
        return carry

    lax.fori_loop(0, 8, step, 0)
    out[...] = acc[...].reshape(R, 16, 128).astype(BF)


def per_device(fam, pair, present, valid, wh, wo, wb, wv, wvo, wlr, wz):
    vm = pl.BlockSpec(memory_space=pltpu.VMEM)
    dma = pltpu.SemaphoreType.DMA
    scratch = [
        pltpu.VMEM((NR, S, R, D), BF),
        pltpu.VMEM((NC, NR, S, R), F32),
        pltpu.VMEM((512, 128), F32),
        pltpu.VMEM((H, 64, 128), BF),
        pltpu.VMEM((H, 64, 128), BF),
        pltpu.VMEM((NR, H, R, 128), BF),
        pltpu.VMEM((S, R, D), BF),
        pltpu.VMEM((S, R, D), F32),
        pltpu.VMEM((NR * R, D), BF),
        pltpu.VMEM((NR * R, D), BF),
        pltpu.VMEM((2, R, D), F32),
        pltpu.VMEM((NC, 64, D), BF),
        pltpu.VMEM((NC, 64, D), BF),
        pltpu.VMEM((2, 1024, 128), F32),
        pltpu.VMEM((2, 1024, 128), F32),
        pltpu.VMEM((2, 1024, 128), F32),
        pltpu.VMEM((NC, 64, D), BF),
        pltpu.VMEM((NC, 64, D), BF),
        pltpu.VMEM((256, 128), F32),
        pltpu.VMEM((256, 128), F32),
        pltpu.VMEM((256, 128), BF),
        pltpu.VMEM((NC, 256, 128), BF),
        pltpu.VMEM((256, 128), BF),
        pltpu.VMEM((8, 256, 128), BF),
        pltpu.VMEM((R, 128), F32),
        pltpu.VMEM((R, 128), F32),
        dma((G, 8)), dma((G, 8)), dma((8,)), dma((8,)), dma((16,)), dma((16,)), dma, dma,
        dma((8,)), dma((8,)), dma((7,)), dma((7,)),
        dma((G, 16)), dma((G, 16)), dma((16,)), dma((16,)), dma((16,)), dma((16,)), dma((8,)), dma((8,)),
    ]
    align, lt, rt, inv = pl.pallas_call(
        msa_kernel,
        out_shape=(
            jax.ShapeDtypeStruct((S, R, D), BF),
            jax.ShapeDtypeStruct((HD * R, 128), BF),
            jax.ShapeDtypeStruct((2048, 128), BF),
            jax.ShapeDtypeStruct((64, 128), F32),
        ),
        in_specs=[vm] * 10,
        out_specs=(vm,) * 4,
        scratch_shapes=scratch,
        compiler_params=pltpu.CompilerParams(has_side_effects=True, vmem_limit_bytes=60 * 1024 * 1024),
        name="msa",
    )(
        fam, pair, present, valid.reshape(NR, R), wh, wo, wb.T, wv, wvo,
        wlr.transpose(0, 2, 1).reshape(64, D),
    )
    pair_out = pl.pallas_call(
        opm_kernel,
        grid=(4,),
        out_shape=jax.ShapeDtypeStruct((R, 64, 128), BF),
        in_specs=[
            pl.BlockSpec((HD * R, 128), lambda i: (0, 0)),
            pl.BlockSpec((512, 128), lambda i: (i, 0)),
            pl.BlockSpec((16, 128), lambda i: (i, 0)),
            pl.BlockSpec((1024, 128), lambda i: (0, 0)),
        ],
        out_specs=pl.BlockSpec((R, 16, 128), lambda i: (0, i, 0)),
        scratch_shapes=[pltpu.VMEM((128, 1024), BF), pltpu.VMEM((R * 16, 128), F32)],
        compiler_params=pltpu.CompilerParams(vmem_limit_bytes=40 * 1024 * 1024),
        name="opm",
    )(lt, rt, inv, wz)
    return align, pair_out


def solution(mesh):
    in_specs = (P("col", "row", None), P("row", "col", None), P("col", "row")) + (P(),) * 8
    out_specs = (P("col", "row", None), P("row", "col", None))
    return jax.shard_map(per_device, mesh=mesh, in_specs=in_specs, out_specs=out_specs, check_vma=False)
```

```python
import jax
import jax.numpy as jnp
from jax import lax
from jax.experimental import pallas as pl
from jax.experimental.pallas import tpu as pltpu
from jax.sharding import PartitionSpec as P

BF = jnp.bfloat16
F32 = jnp.float32
EPS = 1e-05
MASK_BIG = 1000000000.0
MESH = pl.DeviceIdType.MESH

NR = 8
NC = 16
S = 8
R = 128
D = 256
H = 8
HD = 32
G = 2
JT = 8


def norm(x):
    c = x - jnp.mean(x, axis=-1, keepdims=True)
    return c * lax.rsqrt(jnp.mean(c * c, axis=-1, keepdims=True) + EPS)


def dot(a, b):
    return jnp.dot(a, b, preferred_element_type=F32)


def dot_t(a, b):
    return lax.dot_general(a, b, (((1,), (1,)), ((), ())), preferred_element_type=F32)


def sigmoid(x):
    return 1.0 / (1.0 + jnp.exp(-x))


def head_lanes(rows):
    return lax.broadcasted_iota(jnp.int32, (rows, D), 1) // HD


def attend(q, k, v, score_of, step):
    n = q.shape[0]
    lanes = head_lanes(n)
    total = jnp.zeros((n, D), F32)
    for h0 in range(0, H, step):
        heads = range(h0, h0 + step)
        stacked = jnp.concatenate([jnp.where(lanes == h, q, jnp.zeros_like(q)) for h in heads], axis=0)
        raw = dot_t(stacked, k)
        parts, sums = [], []
        for at, h in enumerate(heads):
            s = score_of(h, raw[at * n:(at + 1) * n])
            p = jnp.exp(s - jnp.max(s, axis=-1, keepdims=True))
            sums.append(jnp.sum(p, axis=-1, keepdims=True))
            parts.append(p.astype(BF))
        out = dot(jnp.concatenate(parts, axis=0), v)
        for at, h in enumerate(heads):
            total = jnp.where(lanes == h, out[at * n:(at + 1) * n] * (1.0 / sums[at]), total)
    return total


def msa_kernel(
    fam, pair, present, valid, wh, wo, wb, wv, wvo, wlr, wz,
    align, pair_out,
    ft, nall, livr, lres, lcol, bscr, mine, sib, ball, qs, gs, ks, vs, midf, snd, rcv,
    xf, nf, upf, back_snd, back_rcv, lf, rf, lrcv, rsnd, rrcv, ltt, cmask, inv, ltall, wzt, acc, blocks,
    z_s, z_r, n_s, n_r, lv_s, lv_r, lr_s, lr_r, lc_s, lc_r, sb_s, sb_r, b_s, b_r, bc_s, bc_r,
    m_s, m_r, u_s, u_r, le_s, le_r, lw_s, lw_r, ri_s, ri_r, o_s,
):
    r = lax.axis_index("row")
    c = lax.axis_index("col")
    core = lax.rem(c, 2)
    blk = c // 2
    x, zl = r // 2, lax.rem(r, 2)
    y, zh = c // 4, lax.rem(blk, 2)
    z = zh * 2 + zl
    rz = 2 * x + 1 - zl
    cs = c + 1 - 2 * core
    target = 2 * r + c // 8
    self_row = jnp.where(target == c, r, -1)

    def wrap(i, n):
        return lax.rem(i + n, n)

    def copy(src, dst, ss, rs, row, col):
        return pltpu.make_async_remote_copy(
            src_ref=src, dst_ref=dst, send_sem=ss, recv_sem=rs, device_id=(row, col), device_id_type=MESH
        )

    barrier = pltpu.get_barrier_semaphore()

    def greet(row, col):
        pl.semaphore_signal(barrier, inc=1, device_id=(row, col), device_id_type=MESH)

    for k in range(1, NR):
        greet(wrap(r + k, NR), c)
    for k in range(1, NC):
        greet(r, wrap(c + k, NC))
        greet(rz, wrap(c + k, NC))
    for k in range(8):
        @pl.when(self_row != k)
        def _():
            greet(k, target)

        @pl.when(jnp.logical_or(blk != r, 8 * core + k != c))
        def _():
            greet(blk, 8 * core + k)

    z_copy = copy(fam.at[pl.ds(4 * (1 - zl), 4)], ft.at[zl], z_s, z_r, rz, c)

    xl, xr = wrap(x + 3, 4), wrap(x + 1, 4)
    n_plan = [
        (x, zl, 0, 2, xr), (x, zl, 0, 2, xl), (x, 1 - zl, 0, 2, xr), (x, 1 - zl, 0, 2, xl),
        (xl, zl, 0, 1, xr), (xr, zl, 1, 1, xl), (xl, 1 - zl, 0, 1, xr), (xr, 1 - zl, 1, 1, xl),
    ]

    def nc(g, i):
        xb, zb, lo, n, to = n_plan[i]
        ref = nall.at[xb, zb, pl.ds(2 * g + lo, n)]
        return copy(ref, ref, n_s.at[g, i], n_r.at[g, i], 2 * to + zl, c)

    first = core == 0
    h0 = core * 4

    def at(dp, dq):
        by = wrap(y + jnp.where(first, dq, dp), 4)
        bz = wrap(z + jnp.where(first, dp, dq), 4)
        return by, bz

    def bref(dp, dq, lo, n):
        by, bz = at(dp, dq)
        return ball.at[lax.rem(bz, 2), by * 2 + bz // 2, pl.ds(h0 + lo, n)]

    def bc(slot, dp, dq, lo, n, to_p, to_q):
        ty, tz = at(to_p, to_q)
        ref = bref(dp, dq, lo, n)
        return copy(ref, ref, b_s.at[slot], b_r.at[slot], 2 * x + lax.rem(tz, 2), 4 * ty + 2 * (tz // 2) + core)

    along = (0, 3, 1, 2)

    def b_slot(i):
        if i == 0:
            return bc(0, 0, 0, 0, 4, 1, 0)
        if i == 1:
            return bc(1, 0, 0, 0, 4, 3, 0)
        if i == 2:
            return bc(2, 3, 0, 0, 2, 1, 0)
        if i == 3:
            return bc(3, 1, 0, 2, 2, 3, 0)
        dp = along[(i - 4) % 4]
        if i < 8:
            return bc(i, dp, 0, 0, 4, 0, 1)
        if i < 12:
            return bc(i, dp, 0, 0, 4, 0, 3)
        if i < 16:
            return bc(i, dp, 3, 0, 2, 0, 1)
        return bc(i, dp, 1, 2, 2, 0, 3)

    def b_core(dp, dq):
        ref = bref(dp, dq, 0, 4)
        i = dp * 4 + dq - 1
        return copy(ref, ref, bc_s.at[i], bc_r.at[i], r, cs)

    def b_start(*slots):
        for i in slots:
            b_slot(i).start()

    def b_wait(*slots):
        for i in slots:
            b_slot(i).wait_recv()

    def b_swap(*pairs):
        for p in pairs:
            b_core(*p).start()

    livr[r] = (present[...] * valid[pl.ds(r, 1), :]).astype(F32)
    ft[zl] = fam[pl.ds(4 * zl, 4)]
    for s in range(4):
        nall[x, zl, s] = norm(ft[zl, s].astype(F32)).astype(BF)
    pl.semaphore_wait(barrier, jnp.where(target == c, 51, 53))
    z_copy.start()
    for i in (0, 1):
        for g in range(G):
            nc(g, i).start()

    def lv(k):
        return copy(livr.at[r], livr.at[r], lv_s.at[k], lv_r.at[k], wrap(r + k, NR), c)

    for k in range(1, NR):
        lv(k).start()

    def bias_step(t, carry):
        lo = pair[pl.ds(t * 8, 8)].astype(F32)
        hi = pair[pl.ds(64 + t * 8, 8)].astype(F32)
        rows = norm(jnp.concatenate([lo, hi], axis=1).reshape(1024, 128)).astype(BF)
        b = dot_t(wb[...], rows)
        for i in range(8):
            bscr[pl.ds(t * 64 + i * 8, 8), :] = b[:, i * 128:(i + 1) * 128]
        return carry

    lax.fori_loop(0, 8, bias_step, 0)
    for h in range(H):
        mine[h] = bscr[pl.ds(h, 64, stride=8), :].astype(BF)
    sib_copy = copy(mine, sib, sb_s, sb_r, r, cs)
    sib_copy.start()

    z_copy.wait_recv()
    for s in range(4):
        nall[x, 1 - zl, s] = norm(ft[1 - zl, s].astype(F32)).astype(BF)
    for i in (2, 3):
        for g in range(G):
            nc(g, i).start()

    sib_copy.wait_recv()
    low = lax.broadcasted_iota(jnp.int32, (64, 128), 1) < 64
    for h in range(H):
        a = mine[h].astype(F32)
        b = sib[h].astype(F32)
        left_part = jnp.where(first, a, b)
        right_part = jnp.where(first, b, a)
        ball[zl, blk, h, 0:64, :] = jnp.where(low, left_part, pltpu.roll(right_part, 64, 1)).astype(BF)
        ball[zl, blk, h, 64:128, :] = jnp.where(low, pltpu.roll(left_part, 64, 1), right_part).astype(BF)
    b_start(0, 1, 4, 8)
    for g in range(G):
        for i in (0, 1):
            nc(g, i).wait_recv()
        for i in (4, 5):
            nc(g, i).start()

    for zb in range(2):
        for s in range(4):
            rows = nall[x, zb, s]
            qs[s, zb * R:(zb + 1) * R, :] = (dot(rows, wh[0]) * (HD ** -0.5)).astype(BF)
            gs[s, zb * R:(zb + 1) * R, :] = sigmoid(dot(rows, wh[3]))

    b_wait(0, 1)
    b_start(2, 3, 5, 9, 6, 10)
    b_swap((3, 0), (1, 0))
    b_wait(4, 8)
    b_start(12, 16)
    b_swap((0, 3), (0, 1))
    for g in range(G):
        for i in (2, 3):
            nc(g, i).wait_recv()
        for i in (6, 7):
            nc(g, i).start()
    b_wait(2, 3)
    b_start(7, 11)
    b_swap((2, 0))

    for k in range(1, NR):
        lv(k).wait_recv()
    lres[c] = livr[r]
    lcol[c] = livr[blk]

    def lr(k):
        return copy(livr.at[r], lres.at[c], lr_s.at[k], lr_r.at[k], r, wrap(c + k, NC))

    def lc(k):
        to = wrap(c + k, NC)
        return copy(livr.at[to // 2], lcol.at[c], lc_s.at[k], lc_r.at[k], r, to)

    for k in range(1, NC):
        lr(k).start()
        lc(k).start()

    b_wait(5, 9)
    b_start(13, 17)
    b_swap((3, 3), (3, 1))
    b_wait(6, 10)
    b_start(14, 18)
    b_swap((1, 3), (1, 1))
    b_wait(12, 16)
    b_swap((0, 2))
    b_wait(7, 11)
    b_start(15, 19)
    b_swap((2, 3), (2, 1))
    b_wait(13, 17)
    b_swap((3, 2))
    b_wait(14, 18)
    b_swap((1, 2))
    b_wait(15, 19)
    b_swap((2, 2))
    for g in range(G):
        for i in (4, 5, 6, 7):
            nc(g, i).wait_recv()
    for i in range(1, 16):
        b_core(i // 4, i % 4).wait_recv()

    def mc(g, zb, k):
        to = wrap(c + k, NC)
        return copy(
            snd.at[zb, to, pl.ds(g * 16, 16)], rcv.at[c, zl, pl.ds(g * 16, 16)],
            m_s.at[g, jnp.where(zb == zl, 0, 1), k], m_r.at[g, jnp.where(zb == zl, 0, 1), k],
            2 * x + zb, to,
        )

    def group(g, carry):
        def row_one(i, carry):
            s = 2 * g + i
            for b in range(NR):
                rows = nall[b // 2, b % 2, s]
                ks[b * R:(b + 1) * R, :] = dot(rows, wh[1]).astype(BF)
                vs[b * R:(b + 1) * R, :] = dot(rows, wh[2]).astype(BF)
            keep = jnp.concatenate([livr[b, pl.ds(4 * zl + s, 1), :] for b in range(NR)], axis=1) > 0.5

            def score(h, raw):
                bias = jnp.concatenate(
                    [jnp.concatenate([ball[zb, b, h] for b in range(NR)], axis=1) for zb in range(2)], axis=0
                )
                return jnp.where(keep, raw + bias.astype(F32), -MASK_BIG)

            o = attend(qs[s], ks[...], vs[...], score, 1)
            delta = dot((gs[s] * o).astype(BF), wo[...])
            for zb in range(2):
                midf[i, zb] = ft[zb, s].astype(F32) + delta[zb * R:(zb + 1) * R]
            return carry

        lax.fori_loop(0, 2, row_one, 0)
        for zb in range(2):
            for t in range(NC):
                two = jnp.concatenate([midf[i, zb, t * 8:(t + 1) * 8, :] for i in range(2)], axis=0)
                snd[zb, t, pl.ds(pl.multiple_of(g * 16, 16), 16), :] = two.astype(BF)
        for k in range(NC):
            mc(g, 1 - zl, k).start()
            if k > 0:
                mc(g, zl, k).start()
        return carry

    lax.fori_loop(0, G, group, 0)
    rcv[c, zl] = snd[zl, c]

    for k in range(1, NC):
        lr(k).wait_recv()
        lc(k).wait_recv()
    by_res = lres[...].reshape(R, R).T
    cmask[...] = by_res
    ltt[...] = lcol[...].reshape(R, R).T
    right_live = ltt[pl.ds(pl.multiple_of(core * 64, 64), 64), :]
    inv[...] = 1.0 / jnp.maximum(dot_t(right_live.astype(BF), by_res.astype(BF)), 1.0)
    wzt[...] = wz[...].astype(F32).T.astype(BF)
    for g in range(G):
        for k in range(NC):
            mc(g, 1 - zl, k).wait_recv()
            if k > 0:
                mc(g, zl, k).wait_recv()

    def col_norm(t, carry):
        mid = rcv[t].reshape(64, D).astype(F32)
        rows = pl.ds(pl.multiple_of(t * 64, 64), 64)
        normed = norm(mid)
        for i in range(2):
            xf[i, rows, :] = mid[:, i * 128:(i + 1) * 128]
            nf[i, rows, :] = normed[:, i * 128:(i + 1) * 128]
        return carry

    lax.fori_loop(0, NC, col_norm, 0)

    def col_one(b, carry):
        every = pl.ds(b, R, stride=8)
        rows = jnp.concatenate([nf[i, every, :] for i in range(2)], axis=1).astype(BF)
        q = (dot(rows, wv[0]) * (HD ** -0.5)).astype(BF)
        k = dot(rows, wv[1]).astype(BF)
        v = dot(rows, wv[2]).astype(BF)
        gate = sigmoid(dot(rows, wv[3]))
        row = cmask[pl.ds(c * 8 + b, 1), :]

        def score(h, raw):
            return jnp.where(row > 0.5, raw, -MASK_BIG)

        o = attend(q, k, v, score, 2)
        up = jnp.concatenate([xf[i, every, :] for i in range(2)], axis=1) + dot((gate * o).astype(BF), wvo[...])
        up = up.astype(BF).astype(F32)
        for i in range(2):
            upf[i, every, :] = up[:, i * 128:(i + 1) * 128]
        both = dot_t(wlr[...], norm(up).astype(BF)) * row
        lf[pl.ds(b, HD, stride=8), :] = both[:HD]
        rf[pl.ds(pl.multiple_of(b * HD, HD), HD), :] = both[HD:]
        return carry

    lax.fori_loop(0, 8, col_one, 0)
    lrcv[c] = lf[...].astype(BF)
    rsnd[...] = rf[...].astype(BF)

    cz = c + 2 - 4 * zh
    cl, cr = wrap(c + 12, NC), wrap(c + 4, NC)

    def far(i):
        return i + 2 - 4 * lax.rem(i // 2, 2)

    l_plan = [
        (c, 0, 256, cz), (c, 0, 256, cr), (c, 0, 256, cl), (far(c), 0, 256, cr), (far(c), 0, 256, cl),
        (cl, 0, 128, cr), (cr, 128, 128, cl), (far(cl), 0, 128, cr), (far(cr), 128, 128, cl),
    ]

    def lslot(i):
        owner, lo, n, to = l_plan[i]
        ref = lrcv.at[owner, pl.ds(lo, n)]
        return copy(ref, ref, le_s.at[i], le_r.at[i], r, to)

    def lswap(i):
        ref = lrcv.at[wrap(c + 2 * i, NC)]
        return copy(ref, ref, lw_s.at[i], lw_r.at[i], r, cs)

    place = lax.rem(c, 8)

    def rcopy(k):
        return copy(rsnd, rrcv.at[place], ri_s.at[k], ri_r.at[place], k, target)

    for i in (0, 1, 2):
        lslot(i).start()
    lswap(0).start()
    for k in range(8):
        @pl.when(self_row != k)
        def _():
            rcopy(k).start()

    @pl.when(target == c)
    def _():
        rrcv[place] = rsnd[...]

    lslot(0).wait_recv()
    for i in (3, 4):
        lslot(i).start()
    for i in (1, 2):
        lslot(i).wait_recv()
    for i in (5, 6):
        lslot(i).start()
    for i in (2, 6):
        lswap(i).start()
    far_at = lax.rem(far(c) - c + NC, NC) // 2
    lswap(far_at).start()
    for i in (3, 4):
        lslot(i).wait_recv()
    for i in (7, 8):
        lslot(i).start()
    near = far_at
    lswap(lax.rem(near + 2, 8)).start()
    lswap(lax.rem(near + 6, 8)).start()
    for i in (5, 6):
        lslot(i).wait_recv()
    lswap(4).start()
    for i in (7, 8):
        lslot(i).wait_recv()
    lswap(lax.rem(near + 4, 8)).start()

    for i in range(2):
        back_snd[:, :, i * 128:(i + 1) * 128] = upf[i].reshape(NC, 64, 128).astype(BF)

    def uc(k):
        to = wrap(c + k, NC)
        return copy(back_snd.at[to], back_rcv.at[c], u_s.at[k], u_r.at[k], r, to)

    for k in range(1, NC):
        uc(k).start()
    back_rcv[c] = back_snd[c]

    for i in range(8):
        lswap(i).wait_recv()
    for i in range(HD):
        ltall[i * R:(i + 1) * R, :] = jnp.concatenate(
            [lrcv[t, i * 8:(i + 1) * 8, :] for t in range(NC)], axis=0
        )
    for k in range(8):
        @pl.when(jnp.logical_or(blk != r, 8 * core + k != c))
        def _():
            copy(rsnd, rrcv.at[k], ri_s.at[k], ri_r.at[k], r, c).wait_recv()

    def out_copy(q):
        return pltpu.make_async_copy(
            blocks.at[lax.rem(q, 2)], pair_out.at[:, pl.ds(pl.multiple_of(q * 16, 16), 16), :], o_s.at[lax.rem(q, 2)]
        )

    def sixteen(q, carry):
        def step(t, carry):
            rows = rrcv[2 * q + t]
            o = dot_t(rows, ltall[...]).astype(BF)
            for j0 in range(0, JT, 2):
                two = jnp.concatenate(
                    [
                        jnp.concatenate(
                            [o[j * HD:(j + 1) * HD, i * R:(i + 1) * R] for i in range(HD)], axis=0
                        )
                        for j in (j0, j0 + 1)
                    ],
                    axis=1,
                )
                prod = dot(wzt[...], two)
                for j in range(2):
                    place = t * JT + j0 + j
                    one = prod[:, j * R:(j + 1) * R] * inv[pl.ds(q * 16 + place, 1), :]
                    acc[pl.ds(place, R, stride=16), :] = one.T
            return carry

        lax.fori_loop(0, 2, step, 0)

        @pl.when(q >= 2)
        def _():
            out_copy(q - 2).wait()

        blocks[lax.rem(q, 2)] = acc[...].reshape(R, 16, 128).astype(BF)
        out_copy(q).start()
        return carry

    lax.fori_loop(0, 4, sixteen, 0)
    for k in range(1, NC):
        uc(k).wait_recv()
    for s in range(S):
        align[s] = jnp.concatenate([back_rcv[t, s * 8:(s + 1) * 8, :] for t in range(NC)], axis=0)
    out_copy(2).wait()
    out_copy(3).wait()

    z_copy.wait_send()
    sib_copy.wait_send()
    for g in range(G):
        for i in range(8):
            nc(g, i).wait_send()
        for k in range(NC):
            mc(g, 1 - zl, k).wait_send()
            if k > 0:
                mc(g, zl, k).wait_send()
    for k in range(1, NR):
        lv(k).wait_send()
    for k in range(1, NC):
        lr(k).wait_send()
        lc(k).wait_send()
        uc(k).wait_send()
    for i in range(20):
        b_slot(i).wait_send()
    for i in range(1, 16):
        b_core(i // 4, i % 4).wait_send()
    for i in range(9):
        lslot(i).wait_send()
    for i in range(8):
        lswap(i).wait_send()
    for k in range(8):
        @pl.when(self_row != k)
        def _():
            rcopy(k).wait_send()


def per_device(fam, pair, present, valid, wh, wo, wb, wv, wvo, wlr, wz):
    vm = pl.BlockSpec(memory_space=pltpu.VMEM)
    dma = pltpu.SemaphoreType.DMA

    def sems(*shape):
        return [dma(shape), dma(shape)]

    scratch = [
        pltpu.VMEM((2, 4, R, D), BF),
        pltpu.VMEM((4, 2, 4, R, D), BF),
        pltpu.VMEM((NR, S, R), F32),
        pltpu.VMEM((NC, S, R), F32),
        pltpu.VMEM((NC, S, R), F32),
        pltpu.VMEM((512, 128), F32),
        pltpu.VMEM((H, 64, 128), BF),
        pltpu.VMEM((H, 64, 128), BF),
        pltpu.VMEM((2, NR, H, R, 128), BF),
        pltpu.VMEM((4, 2 * R, D), BF),
        pltpu.VMEM((4, 2 * R, D), F32),
        pltpu.VMEM((NR * R, D), BF),
        pltpu.VMEM((NR * R, D), BF),
        pltpu.VMEM((2, 2, R, D), F32),
        pltpu.VMEM((2, NC, 32, D), BF),
        pltpu.VMEM((NC, 2, 32, D), BF),
        pltpu.VMEM((2, 1024, 128), F32),
        pltpu.VMEM((2, 1024, 128), F32),
        pltpu.VMEM((2, 1024, 128), F32),
        pltpu.VMEM((NC, 64, D), BF),
        pltpu.VMEM((NC, 64, D), BF),
        pltpu.VMEM((256, 128), F32),
        pltpu.VMEM((256, 128), F32),
        pltpu.VMEM((NC, 256, 128), BF),
        pltpu.VMEM((256, 128), BF),
        pltpu.VMEM((8, 256, 128), BF),
        pltpu.VMEM((R, 128), F32),
        pltpu.VMEM((R, 128), F32),
        pltpu.VMEM((64, 128), F32),
        pltpu.VMEM((HD * R, 128), BF),
        pltpu.VMEM((128, 1024), BF),
        pltpu.VMEM((R * 16, 128), F32),
        pltpu.VMEM((2, R, 16, 128), BF),
        dma, dma, *sems(G, 8), *sems(8), *sems(16), *sems(16), dma, dma, *sems(20), *sems(15),
        *sems(G, 2, 16), *sems(16), *sems(9), *sems(8), *sems(8), dma((2,)),
    ]
    return pl.pallas_call(
        msa_kernel,
        out_shape=(jax.ShapeDtypeStruct((S, R, D), BF), jax.ShapeDtypeStruct((R, 64, 128), BF)),
        in_specs=[vm] * 11,
        out_specs=(vm, pl.BlockSpec(memory_space=pl.ANY)),
        scratch_shapes=scratch,
        compiler_params=pltpu.CompilerParams(
            has_side_effects=True, collective_id=0, vmem_limit_bytes=60 * 1024 * 1024
        ),
        name="msa",
    )(
        fam, pair, present, valid.reshape(NR, R), wh, wo, wb.T, wv, wvo,
        wlr.transpose(0, 2, 1).reshape(64, D), wz,
    )


def solution(mesh):
    in_specs = (P("col", "row", None), P("row", "col", None), P("col", "row")) + (P(),) * 8
    out_specs = (P("col", "row", None), P("row", "col", None))
    return jax.shard_map(per_device, mesh=mesh, in_specs=in_specs, out_specs=out_specs, check_vma=False)
```

```python
import jax
import jax.numpy as jnp
from jax import lax
from jax.experimental import pallas as pl
from jax.experimental.pallas import tpu as pltpu
from jax.sharding import PartitionSpec as P

BF = jnp.bfloat16
F32 = jnp.float32
EPS = 1e-05
MASK_BIG = 1000000000.0
MESH = pl.DeviceIdType.MESH

NR = 8
NC = 16
S = 8
R = 128
D = 256
H = 8
HD = 32
G = 2
NB = 4


def norm(x):
    c = x - jnp.mean(x, axis=-1, keepdims=True)
    return c * lax.rsqrt(jnp.mean(c * c, axis=-1, keepdims=True) + EPS)


def dot(a, b):
    return jnp.dot(a, b, preferred_element_type=F32)


def dot_t(a, b):
    return lax.dot_general(a, b, (((1,), (1,)), ((), ())), preferred_element_type=F32)


def sigmoid(x):
    return 1.0 / (1.0 + jnp.exp(-x))


def head_lanes(rows):
    return lax.broadcasted_iota(jnp.int32, (rows, D), 1) // HD


def attend(q, k, v, score_of, step):
    n = q.shape[0]
    lanes = head_lanes(n)
    total = jnp.zeros((n, D), F32)
    for h0 in range(0, H, step):
        heads = range(h0, h0 + step)
        stacked = jnp.concatenate([jnp.where(lanes == h, q, jnp.zeros_like(q)) for h in heads], axis=0)
        raw = dot_t(stacked, k)
        parts, sums = [], []
        for at, h in enumerate(heads):
            s = score_of(h, raw[at * n:(at + 1) * n])
            p = jnp.exp(s - jnp.max(s, axis=-1, keepdims=True))
            sums.append(jnp.sum(p, axis=-1, keepdims=True))
            parts.append(p.astype(BF))
        out = dot(jnp.concatenate(parts, axis=0), v)
        for at, h in enumerate(heads):
            total = jnp.where(lanes == h, out[at * n:(at + 1) * n] * (1.0 / sums[at]), total)
    return total


def msa_kernel(
    fam, pair, present, valid, wh, wo, wb, wv, wvo, wlr, wz,
    align, pair_out,
    ft, nall, livr, lres, lcol, bscr, mine, sib, ball, qs, gs, ks, vs, midf, cqs, cks, cvs, cgs, cos, snd, rcv,
    xf, nf, upf, back_snd, back_rcv, lf, rf, lrcv, rsnd, rrcv, ltt, cmask, inv, ltall, wzt, acc, blocks,
    z_s, z_r, n_s, n_r, lv_s, lv_r, lr_s, lr_r, lc_s, lc_r, sb_s, sb_r, b_s, b_r, bc_s, bc_r,
    m_s, m_r, u_s, u_r, le_s, le_r, lw_s, lw_r, ri_s, ri_r, o_s,
):
    r = lax.axis_index("row")
    c = lax.axis_index("col")
    core = lax.rem(c, 2)
    blk = c // 2
    x, zl = r // 2, lax.rem(r, 2)
    y, zh = c // 4, lax.rem(blk, 2)
    z = zh * 2 + zl
    rz = 2 * x + 1 - zl
    cs = c + 1 - 2 * core
    target = 2 * r + c // 8
    self_row = jnp.where(target == c, r, -1)

    def wrap(i, n):
        return lax.rem(i + n, n)

    def copy(src, dst, ss, rs, row, col):
        return pltpu.make_async_remote_copy(
            src_ref=src, dst_ref=dst, send_sem=ss, recv_sem=rs, device_id=(row, col), device_id_type=MESH
        )

    barrier = pltpu.get_barrier_semaphore()

    def greet(row, col):
        pl.semaphore_signal(barrier, inc=1, device_id=(row, col), device_id_type=MESH)

    for k in range(1, NR):
        greet(wrap(r + k, NR), c)
    for k in range(1, NC):
        greet(r, wrap(c + k, NC))
        greet(rz, wrap(c + k, NC))
    for k in range(8):
        @pl.when(self_row != k)
        def _():
            greet(k, target)

        @pl.when(jnp.logical_or(blk != r, 8 * core + k != c))
        def _():
            greet(blk, 8 * core + k)

    def zc(g):
        src = fam.at[pl.ds(4 * (1 - zl) + 2 * g, 2)]
        return copy(src, ft.at[zl, pl.ds(2 * g, 2)], z_s.at[g], z_r.at[g], rz, c)

    xl, xr = wrap(x + 3, 4), wrap(x + 1, 4)
    n_plan = [
        (x, zl, 0, 2, xr), (x, zl, 0, 2, xl), (x, 1 - zl, 0, 2, xr), (x, 1 - zl, 0, 2, xl),
        (xl, zl, 0, 1, xr), (xr, zl, 1, 1, xl), (xl, 1 - zl, 0, 1, xr), (xr, 1 - zl, 1, 1, xl),
    ]

    def nc(g, i):
        xb, zb, lo, n, to = n_plan[i]
        ref = nall.at[xb, zb, pl.ds(2 * g + lo, n)]
        return copy(ref, ref, n_s.at[g, i], n_r.at[g, i], 2 * to + zl, c)

    first = core == 0
    h0 = core * 4

    def at(dp, dq):
        by = wrap(y + jnp.where(first, dq, dp), 4)
        bz = wrap(z + jnp.where(first, dp, dq), 4)
        return by, bz

    def bref(dp, dq, lo, n):
        by, bz = at(dp, dq)
        return ball.at[lax.rem(bz, 2), by * 2 + bz // 2, pl.ds(h0 + lo, n)]

    def bc(slot, dp, dq, lo, n, to_p, to_q):
        ty, tz = at(to_p, to_q)
        ref = bref(dp, dq, lo, n)
        return copy(ref, ref, b_s.at[slot], b_r.at[slot], 2 * x + lax.rem(tz, 2), 4 * ty + 2 * (tz // 2) + core)

    along = (0, 3, 1, 2)

    def b_slot(i):
        if i == 0:
            return bc(0, 0, 0, 0, 4, 1, 0)
        if i == 1:
            return bc(1, 0, 0, 0, 4, 3, 0)
        if i == 2:
            return bc(2, 3, 0, 0, 2, 1, 0)
        if i == 3:
            return bc(3, 1, 0, 2, 2, 3, 0)
        dp = along[(i - 4) % 4]
        if i < 8:
            return bc(i, dp, 0, 0, 4, 0, 1)
        if i < 12:
            return bc(i, dp, 0, 0, 4, 0, 3)
        if i < 16:
            return bc(i, dp, 3, 0, 2, 0, 1)
        return bc(i, dp, 1, 2, 2, 0, 3)

    def b_core(dp, dq):
        ref = bref(dp, dq, 0, 4)
        i = dp * 4 + dq - 1
        return copy(ref, ref, bc_s.at[i], bc_r.at[i], r, cs)

    def b_start(*slots):
        for i in slots:
            b_slot(i).start()

    def b_wait(*slots):
        for i in slots:
            b_slot(i).wait_recv()

    def b_swap(*pairs):
        for p in pairs:
            b_core(*p).start()

    livr[r] = (present[...] * valid[pl.ds(r, 1), :]).astype(F32)
    ft[zl] = fam[pl.ds(4 * zl, 4)]
    for s in range(4):
        nall[x, zl, s] = norm(ft[zl, s].astype(F32)).astype(BF)
    pl.semaphore_wait(barrier, jnp.where(target == c, 51, 53))
    for g in range(G):
        zc(g).start()
        for i in (0, 1):
            nc(g, i).start()

    def lv(k):
        return copy(livr.at[r], livr.at[r], lv_s.at[k], lv_r.at[k], wrap(r + k, NR), c)

    for k in range(1, NR):
        lv(k).start()

    def bias_step(t, carry):
        lo = pair[pl.ds(t * 8, 8)].astype(F32)
        hi = pair[pl.ds(64 + t * 8, 8)].astype(F32)
        rows = norm(jnp.concatenate([lo, hi], axis=1).reshape(1024, 128)).astype(BF)
        b = dot_t(wb[...], rows)
        for i in range(8):
            bscr[pl.ds(t * 64 + i * 8, 8), :] = b[:, i * 128:(i + 1) * 128]
        return carry

    lax.fori_loop(0, 8, bias_step, 0)
    for h in range(H):
        mine[h] = bscr[pl.ds(h, 64, stride=8), :].astype(BF)
    sib_copy = copy(mine, sib, sb_s, sb_r, r, cs)
    sib_copy.start()

    for g in range(G):
        zc(g).wait_recv()
        for s in (2 * g, 2 * g + 1):
            nall[x, 1 - zl, s] = norm(ft[1 - zl, s].astype(F32)).astype(BF)
        for i in (2, 3):
            nc(g, i).start()

    sib_copy.wait_recv()
    low = lax.broadcasted_iota(jnp.int32, (64, 128), 1) < 64
    for h in range(H):
        a = mine[h].astype(F32)
        b = sib[h].astype(F32)
        left_part = jnp.where(first, a, b)
        right_part = jnp.where(first, b, a)
        ball[zl, blk, h, 0:64, :] = jnp.where(low, left_part, pltpu.roll(right_part, 64, 1)).astype(BF)
        ball[zl, blk, h, 64:128, :] = jnp.where(low, pltpu.roll(left_part, 64, 1), right_part).astype(BF)
    b_start(0, 1, 4, 8)

    def pass_on(g, i):
        for k in (i, i + 1):
            nc(g, k).wait_recv()
        for k in (i + 4, i + 5):
            nc(g, k).start()

    pass_on(0, 0)

    for zb in range(2):
        for s in range(4):
            rows = nall[x, zb, s]
            qs[s, zb * R:(zb + 1) * R, :] = (dot(rows, wh[0]) * (HD ** -0.5)).astype(BF)
            gs[s, zb * R:(zb + 1) * R, :] = sigmoid(dot(rows, wh[3]))

    b_wait(0, 1)
    b_start(2, 3, 5, 9, 6, 10)
    b_swap((3, 0), (1, 0))
    pass_on(0, 2)
    b_wait(4, 8)
    b_start(12, 16)
    b_swap((0, 3), (0, 1))
    pass_on(1, 0)
    b_wait(2, 3)
    b_start(7, 11)
    b_swap((2, 0))
    pass_on(1, 2)

    for k in range(1, NR):
        lv(k).wait_recv()
    lres[c] = livr[r]
    lcol[c] = livr[blk]

    def lr(k):
        return copy(livr.at[r], lres.at[c], lr_s.at[k], lr_r.at[k], r, wrap(c + k, NC))

    def lc(k):
        to = wrap(c + k, NC)
        return copy(livr.at[to // 2], lcol.at[c], lc_s.at[k], lc_r.at[k], r, to)

    for k in range(1, NC):
        lr(k).start()
        lc(k).start()

    b_wait(5, 9)
    b_start(13, 17)
    b_swap((3, 3), (3, 1))
    b_wait(6, 10)
    b_start(14, 18)
    b_swap((1, 3), (1, 1))
    b_wait(12, 16)
    b_swap((0, 2))
    b_wait(7, 11)
    b_start(15, 19)
    b_swap((2, 3), (2, 1))
    b_wait(13, 17)
    b_swap((3, 2))
    b_wait(14, 18)
    b_swap((1, 2))
    b_wait(15, 19)
    b_swap((2, 2))

    def keys_values(g):
        for i in (4, 5, 6, 7):
            nc(g, i).wait_recv()
        for s in (2 * g, 2 * g + 1):
            for b in range(NR):
                rows = nall[b // 2, b % 2, s]
                ks[s, b * R:(b + 1) * R, :] = dot(rows, wh[1]).astype(BF)
                vs[s, b * R:(b + 1) * R, :] = dot(rows, wh[2]).astype(BF)

    keys_values(0)
    for i in range(1, 16):
        b_core(i // 4, i % 4).wait_recv()

    def mc(g, zb, k):
        to = wrap(c + k, NC)
        return copy(
            snd.at[zb, to, pl.ds(g * 16, 16)], rcv.at[c, zl, pl.ds(g * 16, 16)],
            m_s.at[g, jnp.where(zb == zl, 0, 1), k], m_r.at[g, jnp.where(zb == zl, 0, 1), k],
            2 * x + zb, to,
        )

    def group(g):
        def row_one(i, carry):
            s = 2 * g + i
            keep = jnp.concatenate([livr[b, pl.ds(4 * zl + s, 1), :] for b in range(NR)], axis=1) > 0.5

            def score(h, raw):
                bias = jnp.concatenate(
                    [jnp.concatenate([ball[zb, b, h] for b in range(NR)], axis=1) for zb in range(2)], axis=0
                )
                return jnp.where(keep, raw + bias.astype(F32), -MASK_BIG)

            o = attend(qs[s], ks[s], vs[s], score, 1)
            delta = dot((gs[s] * o).astype(BF), wo[...])
            for zb in range(2):
                midf[i, zb] = ft[zb, s].astype(F32) + delta[zb * R:(zb + 1) * R]
            return carry

        lax.fori_loop(0, 2, row_one, 0)
        for zb in range(2):
            for t in range(NC):
                two = jnp.concatenate([midf[i, zb, t * 8:(t + 1) * 8, :] for i in range(2)], axis=0)
                snd[zb, t, g * 16:(g + 1) * 16, :] = two.astype(BF)
        for k in range(NC):
            mc(g, 1 - zl, k).start()
            if k > 0:
                mc(g, zl, k).start()

    group(0)
    keys_values(1)
    group(1)
    rcv[c, zl] = snd[zl, c]

    for k in range(1, NC):
        lr(k).wait_recv()
        lc(k).wait_recv()
    by_res = lres[...].reshape(R, R).T
    cmask[...] = by_res
    ltt[...] = lcol[...].reshape(R, R).T
    right_live = ltt[pl.ds(pl.multiple_of(core * 64, 64), 64), :]
    inv[...] = 1.0 / jnp.maximum(dot_t(right_live.astype(BF), by_res.astype(BF)), 1.0)
    wzt[...] = wz[...].astype(F32).T.astype(BF)
    for g in range(G):
        for k in range(NC):
            mc(g, 1 - zl, k).wait_recv()
            if k > 0:
                mc(g, zl, k).wait_recv()

    def col_norm(t, carry):
        mid = rcv[t].reshape(64, D).astype(F32)
        rows = pl.ds(pl.multiple_of(t * 64, 64), 64)
        normed = norm(mid)
        for i in range(2):
            xf[i, rows, :] = mid[:, i * 128:(i + 1) * 128]
            nf[i, rows, :] = normed[:, i * 128:(i + 1) * 128]
        return carry

    lax.fori_loop(0, NC, col_norm, 0)

    def rows_of(ref, p):
        return jnp.concatenate(
            [
                jnp.concatenate([ref[i, pl.ds(p * NB + b, R, stride=8), :] for i in range(2)], axis=1)
                for b in range(NB)
            ],
            axis=0,
        )

    def col_half(p):
        rows = rows_of(nf, p).astype(BF)
        cqs[...] = (dot(rows, wv[0]) * (HD ** -0.5)).astype(BF)
        cks[...] = dot(rows, wv[1]).astype(BF)
        cvs[...] = dot(rows, wv[2]).astype(BF)
        cgs[...] = sigmoid(dot(rows, wv[3]))
        for b in range(NB):
            row = cmask[pl.ds(c * 8 + p * NB + b, 1), :]
            span = slice(b * R, (b + 1) * R)

            def score(h, raw):
                return jnp.where(row > 0.5, raw, -MASK_BIG)

            o = attend(cqs[span, :], cks[span, :], cvs[span, :], score, 2)
            cos[span, :] = (cgs[span, :] * o).astype(BF)
        up = (rows_of(xf, p) + dot(cos[...], wvo[...])).astype(BF).astype(F32)
        both = dot_t(wlr[...], norm(up).astype(BF))
        for b in range(NB):
            span = slice(b * R, (b + 1) * R)
            for i in range(2):
                upf[i, pl.ds(p * NB + b, R, stride=8), :] = up[span, i * 128:(i + 1) * 128]
            one = both[:, span] * cmask[pl.ds(c * 8 + p * NB + b, 1), :]
            lf[pl.ds(p * 128 + b, HD, stride=NB), :] = one[:HD]
            rf[(p * NB + b) * HD:(p * NB + b + 1) * HD, :] = one[HD:]
        lrcv[c, p * 128:(p + 1) * 128, :] = lf[p * 128:(p + 1) * 128, :].astype(BF)
        rsnd[p * 128:(p + 1) * 128, :] = rf[p * 128:(p + 1) * 128, :].astype(BF)

    cz = c + 2 - 4 * zh
    cl, cr = wrap(c + 12, NC), wrap(c + 4, NC)

    def far(i):
        return i + 2 - 4 * lax.rem(i // 2, 2)

    l_plan = [
        (c, 0, 128, cz), (c, 0, 128, cr), (c, 0, 128, cl), (far(c), 0, 128, cr), (far(c), 0, 128, cl),
        (cl, 0, 64, cr), (cr, 64, 64, cl), (far(cl), 0, 64, cr), (far(cr), 64, 64, cl),
    ]
    near = lax.rem(far(c) - c + NC, NC) // 2

    def lslot(p, i):
        owner, lo, n, to = l_plan[i]
        ref = lrcv.at[owner, pl.ds(p * 128 + lo, n)]
        return copy(ref, ref, le_s.at[p, i], le_r.at[p, i], r, to)

    def lswap(p, i):
        ref = lrcv.at[wrap(c + 2 * i, NC), pl.ds(p * 128, 128)]
        return copy(ref, ref, lw_s.at[p, i], lw_r.at[p, i], r, cs)

    place = lax.rem(c, 8)

    def rcopy(p, k):
        span = pl.ds(p * 128, 128)
        return copy(rsnd.at[span], rrcv.at[place, span], ri_s.at[p, k], ri_r.at[p, place], k, target)

    def left_one(p):
        for i in (0, 1, 2):
            lslot(p, i).start()
        lswap(p, 0).start()

    def left_two(p):
        for i in (0, 1, 2):
            lslot(p, i).wait_recv()
        for i in (3, 4, 5, 6):
            lslot(p, i).start()
        lswap(p, near).start()
        lswap(p, 2).start()
        lswap(p, 6).start()

    def left_three(p):
        for i in (3, 4):
            lslot(p, i).wait_recv()
        for i in (7, 8):
            lslot(p, i).start()
        lswap(p, lax.rem(near + 2, 8)).start()
        lswap(p, lax.rem(near + 6, 8)).start()
        for i in (5, 6):
            lslot(p, i).wait_recv()
        lswap(p, 4).start()

    def left_four(p):
        for i in (7, 8):
            lslot(p, i).wait_recv()
        lswap(p, lax.rem(near + 4, 8)).start()

    def right_send(p):
        for k in range(8):
            @pl.when(self_row != k)
            def _():
                rcopy(p, k).start()

    def right_wait(p):
        span = pl.ds(p * 128, 128)
        for k in range(8):
            @pl.when(jnp.logical_or(blk != r, 8 * core + k != c))
            def _():
                copy(rsnd.at[span], rrcv.at[k, span], ri_s.at[p, k], ri_r.at[p, k], r, c).wait_recv()

    col_half(0)
    left_one(0)
    right_send(0)
    col_half(1)
    left_one(1)
    left_two(0)
    left_two(1)
    left_three(0)
    left_three(1)
    right_send(1)

    @pl.when(target == c)
    def _():
        rrcv[place] = rsnd[...]

    left_four(0)
    left_four(1)

    for i in range(2):
        back_snd[:, :, i * 128:(i + 1) * 128] = upf[i].reshape(NC, 64, 128).astype(BF)

    def uc(k):
        to = wrap(c + k, NC)
        return copy(back_snd.at[to], back_rcv.at[c], u_s.at[k], u_r.at[k], r, to)

    for k in range(1, NC):
        uc(k).start()
    back_rcv[c] = back_snd[c]

    for p in range(2):
        for i in range(8):
            lswap(p, i).wait_recv()
    low4 = lax.rem(lax.broadcasted_iota(jnp.int32, (R, 128), 0), 8) < 4
    for m in range(16):
        a = lrcv[:, m * 8:(m + 1) * 8, :].astype(F32).reshape(R, 128)
        b = lrcv[:, 128 + m * 8:128 + (m + 1) * 8, :].astype(F32).reshape(R, 128)
        ltall[2 * m * R:(2 * m + 1) * R, :] = jnp.where(low4, a, pltpu.roll(b, 4, 0)).astype(BF)
        ltall[(2 * m + 1) * R:(2 * m + 2) * R, :] = jnp.where(low4, pltpu.roll(a, R - 4, 0), b).astype(BF)

    def out_copy(q):
        return pltpu.make_async_copy(
            blocks.at[lax.rem(q, 2)], pair_out.at[:, pl.ds(pl.multiple_of(q * 16, 16), 16), :], o_s.at[lax.rem(q, 2)]
        )

    def eight(q, p):
        rows = jnp.concatenate([rrcv[2 * q + t, p * 128:(p + 1) * 128, :] for t in range(2)], axis=0)
        o = dot_t(rows, ltall[...]).astype(BF)
        for j0 in range(0, 8, 2):
            two = jnp.concatenate(
                [
                    jnp.concatenate([o[j * HD:(j + 1) * HD, i * R:(i + 1) * R] for i in range(HD)], axis=0)
                    for j in (j0, j0 + 1)
                ],
                axis=1,
            )
            prod = dot(wzt[...], two)
            for i in range(2):
                j = q * 16 + (j0 + i) // NB * 8 + p * NB + (j0 + i) % NB
                one = prod[:, i * R:(i + 1) * R] * inv[pl.ds(j, 1), :]
                acc[pl.ds(j, R, stride=64), :] = one.T

    def first_half(q, carry):
        eight(q, 0)
        return carry

    def second_half(q, carry):
        eight(q, 1)

        @pl.when(q >= 2)
        def _():
            out_copy(q - 2).wait()

        for t in range(4):
            @pl.when(q == t)
            def _():
                blocks[t % 2] = acc[...].reshape(R, 64, 128)[:, t * 16:(t + 1) * 16, :].astype(BF)
        out_copy(q).start()
        return carry

    right_wait(0)
    lax.fori_loop(0, 4, first_half, 0)
    right_wait(1)
    lax.fori_loop(0, 4, second_half, 0)
    for k in range(1, NC):
        uc(k).wait_recv()
    for s in range(S):
        align[s] = jnp.concatenate([back_rcv[t, s * 8:(s + 1) * 8, :] for t in range(NC)], axis=0)
    out_copy(2).wait()
    out_copy(3).wait()

    for g in range(G):
        zc(g).wait_send()
    sib_copy.wait_send()
    for g in range(G):
        for i in range(8):
            nc(g, i).wait_send()
        for k in range(NC):
            mc(g, 1 - zl, k).wait_send()
            if k > 0:
                mc(g, zl, k).wait_send()
    for k in range(1, NR):
        lv(k).wait_send()
    for k in range(1, NC):
        lr(k).wait_send()
        lc(k).wait_send()
        uc(k).wait_send()
    for i in range(20):
        b_slot(i).wait_send()
    for i in range(1, 16):
        b_core(i // 4, i % 4).wait_send()
    for p in range(2):
        for i in range(9):
            lslot(p, i).wait_send()
        for i in range(8):
            lswap(p, i).wait_send()
        for k in range(8):
            @pl.when(self_row != k)
            def _():
                rcopy(p, k).wait_send()


def relay_kernel(a, b, a_out, b_out, sem):
    copies = [pltpu.make_async_copy(a, a_out, sem.at[0])]
    for i in range(4):
        rows = pl.ds(i * 32, 32)
        copies.append(pltpu.make_async_copy(b.at[rows], b_out.at[rows], sem.at[1 + i]))
    for cp in copies:
        cp.start()
    for cp in copies:
        cp.wait()


def per_device(fam, pair, present, valid, wh, wo, wb, wv, wvo, wlr, wz):
    vm = pl.BlockSpec(memory_space=pltpu.VMEM)
    dma = pltpu.SemaphoreType.DMA

    def sems(*shape):
        return [dma(shape), dma(shape)]

    scratch = [
        pltpu.VMEM((2, 4, R, D), BF),
        pltpu.VMEM((4, 2, 4, R, D), BF),
        pltpu.VMEM((NR, S, R), F32),
        pltpu.VMEM((NC, S, R), F32),
        pltpu.VMEM((NC, S, R), F32),
        pltpu.VMEM((512, 128), F32),
        pltpu.VMEM((H, 64, 128), BF),
        pltpu.VMEM((H, 64, 128), BF),
        pltpu.VMEM((2, NR, H, R, 128), BF),
        pltpu.VMEM((4, 2 * R, D), BF),
        pltpu.VMEM((4, 2 * R, D), F32),
        pltpu.VMEM((4, NR * R, D), BF),
        pltpu.VMEM((4, NR * R, D), BF),
        pltpu.VMEM((2, 2, R, D), F32),
        pltpu.VMEM((NB * R, D), BF),
        pltpu.VMEM((NB * R, D), BF),
        pltpu.VMEM((NB * R, D), BF),
        pltpu.VMEM((NB * R, D), F32),
        pltpu.VMEM((NB * R, D), BF),
        pltpu.VMEM((2, NC, 32, D), BF),
        pltpu.VMEM((NC, 2, 32, D), BF),
        pltpu.VMEM((2, 1024, 128), F32),
        pltpu.VMEM((2, 1024, 128), F32),
        pltpu.VMEM((2, 1024, 128), F32),
        pltpu.VMEM((NC, 64, D), BF),
        pltpu.VMEM((NC, 64, D), BF),
        pltpu.VMEM((256, 128), F32),
        pltpu.VMEM((256, 128), F32),
        pltpu.VMEM((NC, 256, 128), BF),
        pltpu.VMEM((256, 128), BF),
        pltpu.VMEM((8, 256, 128), BF),
        pltpu.VMEM((R, 128), F32),
        pltpu.VMEM((R, 128), F32),
        pltpu.VMEM((64, 128), F32),
        pltpu.VMEM((HD * R, 128), BF),
        pltpu.VMEM((128, 1024), BF),
        pltpu.VMEM((R * 64, 128), F32),
        pltpu.VMEM((2, R, 16, 128), BF),
        *sems(G), *sems(G, 8), *sems(8), *sems(16), *sems(16), dma, dma, *sems(20), *sems(15),
        *sems(G, 2, 16), *sems(16), *sems(2, 9), *sems(2, 8), *sems(2, 8), dma((2,)),
    ]
    align, pair_out = pl.pallas_call(
        msa_kernel,
        out_shape=(jax.ShapeDtypeStruct((S, R, D), BF), jax.ShapeDtypeStruct((R, 64, 128), BF)),
        in_specs=[vm] * 11,
        out_specs=(vm, pl.BlockSpec(memory_space=pl.ANY)),
        scratch_shapes=scratch,
        compiler_params=pltpu.CompilerParams(
            has_side_effects=True, collective_id=0, vmem_limit_bytes=60 * 1024 * 1024
        ),
        name="msa",
    )(
        fam, pair, present, valid.reshape(NR, R), wh, wo, wb.T, wv, wvo,
        wlr.transpose(0, 2, 1).reshape(64, D), wz,
    )
    anywhere = pl.BlockSpec(memory_space=pl.ANY)
    return pl.pallas_call(
        relay_kernel,
        out_shape=(jax.ShapeDtypeStruct((S, R, D), BF), jax.ShapeDtypeStruct((R, 64, 128), BF)),
        in_specs=[anywhere] * 2,
        out_specs=(anywhere,) * 2,
        scratch_shapes=[dma((5,))],
        compiler_params=pltpu.CompilerParams(vmem_limit_bytes=60 * 1024 * 1024),
        name="relay",
    )(align, pair_out)


def solution(mesh):
    in_specs = (P("col", "row", None), P("row", "col", None), P("col", "row")) + (P(),) * 8
    out_specs = (P("col", "row", None), P("row", "col", None))
    return jax.shard_map(per_device, mesh=mesh, in_specs=in_specs, out_specs=out_specs, check_vma=False)
```

```python
import jax
import jax.numpy as jnp
from jax import lax
from jax.experimental import pallas as pl
from jax.experimental.pallas import tpu as pltpu
from jax.sharding import PartitionSpec as P

BF = jnp.bfloat16
F32 = jnp.float32
EPS = 1e-05
MASK_BIG = 1000000000.0
MESH = pl.DeviceIdType.MESH

NR = 8
NC = 16
S = 8
R = 128
D = 256
H = 8
HD = 32
G = 2
NB = 4


def norm(x):
    c = x - jnp.mean(x, axis=-1, keepdims=True)
    return c * lax.rsqrt(jnp.mean(c * c, axis=-1, keepdims=True) + EPS)


def dot(a, b):
    return jnp.dot(a, b, preferred_element_type=F32)


def dot_t(a, b):
    return lax.dot_general(a, b, (((1,), (1,)), ((), ())), preferred_element_type=F32)


def sigmoid(x):
    return 1.0 / (1.0 + jnp.exp(-x))


def head_lanes(rows):
    return lax.broadcasted_iota(jnp.int32, (rows, D), 1) // HD


def attend(q, k, v, score_of, step):
    n = q.shape[0]
    lanes = head_lanes(n)
    total = jnp.zeros((n, D), F32)
    for h0 in range(0, H, step):
        heads = range(h0, h0 + step)
        stacked = jnp.concatenate([jnp.where(lanes == h, q, jnp.zeros_like(q)) for h in heads], axis=0)
        raw = dot_t(stacked, k)
        parts, sums = [], []
        for at, h in enumerate(heads):
            s = score_of(h, raw[at * n:(at + 1) * n])
            p = jnp.exp(s - jnp.max(s, axis=-1, keepdims=True))
            sums.append(jnp.sum(p, axis=-1, keepdims=True))
            parts.append(p.astype(BF))
        out = dot(jnp.concatenate(parts, axis=0), v)
        for at, h in enumerate(heads):
            total = jnp.where(lanes == h, out[at * n:(at + 1) * n] * (1.0 / sums[at]), total)
    return total


def msa_kernel(
    fam_in, pair_in, present, valid, wh_in, wo_in, wb, wv_in, wvo_in, wlr, wz_in,
    align, pair_out,
    fam, pair, wh, wo, wv, wvo, wz, ft, nall, livr, lres, lcol, bscr, mine, sib, ball, qs, gs, ks, vs, midf, cqs, cks, cvs, cgs, cos, snd, rcv,
    xf, nf, upf, back_snd, back_rcv, lf, rf, lrcv, rsnd, rrcv, ltt, cmask, inv, ltall, wzt, acc, blocks,
    z_s, z_r, n_s, n_r, lv_s, lv_r, lr_s, lr_r, lc_s, lc_r, sb_s, sb_r, b_s, b_r, bc_s, bc_r,
    m_s, m_r, u_s, u_r, le_s, le_r, lw_s, lw_r, ri_s, ri_r, o_s, in_s,
):
    r = lax.axis_index("row")
    c = lax.axis_index("col")
    core = lax.rem(c, 2)
    blk = c // 2
    x, zl = r // 2, lax.rem(r, 2)
    y, zh = c // 4, lax.rem(blk, 2)
    z = zh * 2 + zl
    rz = 2 * x + 1 - zl
    cs = c + 1 - 2 * core
    target = 2 * r + c // 8
    self_row = jnp.where(target == c, r, -1)

    pairs = [(fam_in, fam), (pair_in, pair), (wh_in, wh), (wo_in, wo), (wv_in, wv), (wvo_in, wvo), (wz_in, wz)]
    loads = [pltpu.make_async_copy(a, b, in_s.at[i]) for i, (a, b) in enumerate(pairs)]
    for cp in loads:
        cp.start()

    def wrap(i, n):
        return lax.rem(i + n, n)

    def copy(src, dst, ss, rs, row, col):
        return pltpu.make_async_remote_copy(
            src_ref=src, dst_ref=dst, send_sem=ss, recv_sem=rs, device_id=(row, col), device_id_type=MESH
        )

    barrier = pltpu.get_barrier_semaphore()

    def greet(row, col):
        pl.semaphore_signal(barrier, inc=1, device_id=(row, col), device_id_type=MESH)

    for k in range(1, NR):
        greet(wrap(r + k, NR), c)
    for k in range(1, NC):
        greet(r, wrap(c + k, NC))
        greet(rz, wrap(c + k, NC))
    for k in range(8):
        @pl.when(self_row != k)
        def _():
            greet(k, target)

        @pl.when(jnp.logical_or(blk != r, 8 * core + k != c))
        def _():
            greet(blk, 8 * core + k)

    def zc(g):
        src = fam.at[pl.ds(4 * (1 - zl) + 2 * g, 2)]
        return copy(src, ft.at[zl, pl.ds(2 * g, 2)], z_s.at[g], z_r.at[g], rz, c)

    xl, xr = wrap(x + 3, 4), wrap(x + 1, 4)
    n_plan = [
        (x, zl, 0, 2, xr), (x, zl, 0, 2, xl), (x, 1 - zl, 0, 2, xr), (x, 1 - zl, 0, 2, xl),
        (xl, zl, 0, 1, xr), (xr, zl, 1, 1, xl), (xl, 1 - zl, 0, 1, xr), (xr, 1 - zl, 1, 1, xl),
    ]

    def nc(g, i):
        xb, zb, lo, n, to = n_plan[i]
        ref = nall.at[xb, zb, pl.ds(2 * g + lo, n)]
        return copy(ref, ref, n_s.at[g, i], n_r.at[g, i], 2 * to + zl, c)

    first = core == 0
    h0 = core * 4

    def at(dp, dq):
        by = wrap(y + jnp.where(first, dq, dp), 4)
        bz = wrap(z + jnp.where(first, dp, dq), 4)
        return by, bz

    def bref(dp, dq, lo, n):
        by, bz = at(dp, dq)
        return ball.at[lax.rem(bz, 2), by * 2 + bz // 2, pl.ds(h0 + lo, n)]

    def bc(slot, dp, dq, lo, n, to_p, to_q):
        ty, tz = at(to_p, to_q)
        ref = bref(dp, dq, lo, n)
        return copy(ref, ref, b_s.at[slot], b_r.at[slot], 2 * x + lax.rem(tz, 2), 4 * ty + 2 * (tz // 2) + core)

    along = (0, 3, 1, 2)

    def b_slot(i):
        if i == 0:
            return bc(0, 0, 0, 0, 4, 1, 0)
        if i == 1:
            return bc(1, 0, 0, 0, 4, 3, 0)
        if i == 2:
            return bc(2, 0, 0, 0, 4, 2, 0)
        if i == 3:
            return bc(3, 2, 0, 0, 4, 0, 2)
        dp = along[(i - 4) % 4]
        if i < 8:
            return bc(i, dp, 0, 0, 4, 0, 1)
        if i < 12:
            return bc(i, dp, 0, 0, 4, 0, 3)
        if i < 15:
            return bc(i, dp, 3, 0, 2, 0, 1)
        return bc(i, dp, 1, 2, 2, 0, 3)

    b_used = [i for i in range(19) if i != 15]

    def b_core(dp, dq):
        ref = bref(dp, dq, 0, 4)
        i = dp * 4 + dq - 1
        return copy(ref, ref, bc_s.at[i], bc_r.at[i], r, cs)

    def b_start(*slots):
        for i in slots:
            b_slot(i).start()

    def b_wait(*slots):
        for i in slots:
            b_slot(i).wait_recv()

    def b_swap(*pairs):
        for p in pairs:
            b_core(*p).start()

    livr[r] = (present[...] * valid[pl.ds(r, 1), :]).astype(F32)
    loads[0].wait()
    ft[zl] = fam[pl.ds(4 * zl, 4)]
    for s in range(4):
        nall[x, zl, s] = norm(ft[zl, s].astype(F32)).astype(BF)
    pl.semaphore_wait(barrier, jnp.where(target == c, 51, 53))
    for g in range(G):
        zc(g).start()
        for i in (0, 1):
            nc(g, i).start()

    def lv(k):
        return copy(livr.at[r], livr.at[r], lv_s.at[k], lv_r.at[k], wrap(r + k, NR), c)

    for k in range(1, NR):
        lv(k).start()

    def bias_step(t, carry):
        lo = pair[pl.ds(t * 8, 8)].astype(F32)
        hi = pair[pl.ds(64 + t * 8, 8)].astype(F32)
        rows = norm(jnp.concatenate([lo, hi], axis=1).reshape(1024, 128)).astype(BF)
        b = dot_t(wb[...], rows)
        for i in range(8):
            bscr[pl.ds(t * 64 + i * 8, 8), :] = b[:, i * 128:(i + 1) * 128]
        return carry

    loads[1].wait()
    lax.fori_loop(0, 8, bias_step, 0)
    for h in range(H):
        mine[h] = bscr[pl.ds(h, 64, stride=8), :].astype(BF)
    sib_copy = copy(mine, sib, sb_s, sb_r, r, cs)
    sib_copy.start()

    def pass_on(g, i):
        for k in (i, i + 1):
            nc(g, k).wait_recv()
        for k in (i + 4, i + 5):
            nc(g, k).start()

    def partner(g):
        zc(g).wait_recv()
        for s in (2 * g, 2 * g + 1):
            nall[x, 1 - zl, s] = norm(ft[1 - zl, s].astype(F32)).astype(BF)
        for i in (2, 3):
            nc(g, i).start()

    def query(zb, s):
        rows = nall[x, zb, s]
        qs[s, pl.ds(pl.multiple_of(zb * R, R), R), :] = (dot(rows, wh[0]) * (HD ** -0.5)).astype(BF)
        gs[s, pl.ds(pl.multiple_of(zb * R, R), R), :] = sigmoid(dot(rows, wh[3]))

    sib_copy.wait_recv()
    low = lax.broadcasted_iota(jnp.int32, (64, 128), 1) < 64
    for h in range(H):
        a = mine[h].astype(F32)
        b = sib[h].astype(F32)
        left_part = jnp.where(first, a, b)
        right_part = jnp.where(first, b, a)
        ball[zl, blk, h, 0:64, :] = jnp.where(low, left_part, pltpu.roll(right_part, 64, 1)).astype(BF)
        ball[zl, blk, h, 64:128, :] = jnp.where(low, pltpu.roll(left_part, 64, 1), right_part).astype(BF)
    b_start(0, 1, 2, 4, 8)
    partner(0)
    partner(1)
    loads[2].wait()
    query(zl, 0)
    pass_on(0, 0)
    b_wait(0, 1)
    b_start(5, 9, 6, 10)
    b_swap((3, 0), (1, 0))
    b_wait(2)
    b_start(7, 11, 3)
    b_swap((2, 0))
    query(zl, 1)
    b_wait(4, 8)
    b_start(12, 16)
    b_swap((0, 3), (0, 1))
    pass_on(0, 2)
    query(zl, 2)
    pass_on(1, 0)
    query(zl, 3)
    b_wait(5, 9)
    b_start(13, 17)
    b_swap((3, 3), (3, 1))
    query(1 - zl, 0)
    b_wait(6, 10)
    b_start(14, 18)
    b_swap((1, 3), (1, 1))
    pass_on(1, 2)

    for k in range(1, NR):
        lv(k).wait_recv()
    lres[c] = livr[r]
    lcol[c] = livr[blk]

    def lr(k):
        return copy(livr.at[r], lres.at[c], lr_s.at[k], lr_r.at[k], r, wrap(c + k, NC))

    def lc(k):
        to = wrap(c + k, NC)
        return copy(livr.at[to // 2], lcol.at[c], lc_s.at[k], lc_r.at[k], r, to)

    for k in range(1, NC):
        lr(k).start()
        lc(k).start()

    for s in (1, 2, 3):
        query(1 - zl, s)
    b_wait(12, 16)
    b_swap((0, 2))
    b_wait(7, 11)
    b_swap((2, 3), (2, 1))

    def keys_values(g):
        for i in (4, 5, 6, 7):
            nc(g, i).wait_recv()
        for s in (2 * g, 2 * g + 1):
            for b in range(NR):
                rows = nall[b // 2, b % 2, s]
                ks[s, b * R:(b + 1) * R, :] = dot(rows, wh[1]).astype(BF)
                vs[s, b * R:(b + 1) * R, :] = dot(rows, wh[2]).astype(BF)

    keys_values(0)
    b_wait(13, 17)
    b_swap((3, 2))
    b_wait(14, 18)
    b_swap((1, 2))
    b_wait(3)
    b_swap((2, 2))
    loads[3].wait()
    for i in range(1, 16):
        b_core(i // 4, i % 4).wait_recv()

    def mc(g, zb, k):
        to = wrap(c + k, NC)
        return copy(
            snd.at[zb, to, pl.ds(g * 16, 16)], rcv.at[c, zl, pl.ds(g * 16, 16)],
            m_s.at[g, jnp.where(zb == zl, 0, 1), k], m_r.at[g, jnp.where(zb == zl, 0, 1), k],
            2 * x + zb, to,
        )

    def group(g):
        def row_one(i, carry):
            s = 2 * g + i
            keep = jnp.concatenate([livr[b, pl.ds(4 * zl + s, 1), :] for b in range(NR)], axis=1) > 0.5

            def score(h, raw):
                bias = jnp.concatenate(
                    [jnp.concatenate([ball[zb, b, h] for b in range(NR)], axis=1) for zb in range(2)], axis=0
                )
                return jnp.where(keep, raw + bias.astype(F32), -MASK_BIG)

            o = attend(qs[s], ks[s], vs[s], score, 1)
            delta = dot((gs[s] * o).astype(BF), wo[...])
            for zb in range(2):
                midf[i, zb] = ft[zb, s].astype(F32) + delta[zb * R:(zb + 1) * R]
            return carry

        lax.fori_loop(0, 2, row_one, 0)
        for zb in range(2):
            for t in range(NC):
                two = jnp.concatenate([midf[i, zb, t * 8:(t + 1) * 8, :] for i in range(2)], axis=0)
                snd[zb, t, g * 16:(g + 1) * 16, :] = two.astype(BF)
        for k in range(NC):
            mc(g, 1 - zl, k).start()
            if k > 0:
                mc(g, zl, k).start()

    group(0)
    keys_values(1)
    group(1)
    rcv[c, zl] = snd[zl, c]

    for k in range(1, NC):
        lr(k).wait_recv()
        lc(k).wait_recv()
    by_res = lres[...].reshape(R, R).T
    cmask[...] = by_res
    ltt[...] = lcol[...].reshape(R, R).T
    right_live = ltt[pl.ds(pl.multiple_of(core * 64, 64), 64), :]
    inv[...] = 1.0 / jnp.maximum(dot_t(right_live.astype(BF), by_res.astype(BF)), 1.0)
    for i in (4, 5, 6):
        loads[i].wait()
    wzt[...] = wz[...].astype(F32).T.astype(BF)
    for g in range(G):
        for k in range(NC):
            mc(g, 1 - zl, k).wait_recv()
            if k > 0:
                mc(g, zl, k).wait_recv()

    def col_norm(t, carry):
        mid = rcv[t].reshape(64, D).astype(F32)
        rows = pl.ds(pl.multiple_of(t * 64, 64), 64)
        normed = norm(mid)
        for i in range(2):
            xf[i, rows, :] = mid[:, i * 128:(i + 1) * 128]
            nf[i, rows, :] = normed[:, i * 128:(i + 1) * 128]
        return carry

    lax.fori_loop(0, NC, col_norm, 0)

    def rows_of(ref, p):
        return jnp.concatenate(
            [
                jnp.concatenate([ref[i, pl.ds(p * NB + b, R, stride=8), :] for i in range(2)], axis=1)
                for b in range(NB)
            ],
            axis=0,
        )

    def col_half(p):
        rows = rows_of(nf, p).astype(BF)
        cqs[...] = (dot(rows, wv[0]) * (HD ** -0.5)).astype(BF)
        cks[...] = dot(rows, wv[1]).astype(BF)
        cvs[...] = dot(rows, wv[2]).astype(BF)
        cgs[...] = sigmoid(dot(rows, wv[3]))
        for b in range(NB):
            row = cmask[pl.ds(c * 8 + p * NB + b, 1), :]
            span = slice(b * R, (b + 1) * R)

            def score(h, raw):
                return jnp.where(row > 0.5, raw, -MASK_BIG)

            o = attend(cqs[span, :], cks[span, :], cvs[span, :], score, 2)
            cos[span, :] = (cgs[span, :] * o).astype(BF)
        up = (rows_of(xf, p) + dot(cos[...], wvo[...])).astype(BF).astype(F32)
        both = dot_t(wlr[...], norm(up).astype(BF))
        for b in range(NB):
            span = slice(b * R, (b + 1) * R)
            for i in range(2):
                upf[i, pl.ds(p * NB + b, R, stride=8), :] = up[span, i * 128:(i + 1) * 128]
            one = both[:, span] * cmask[pl.ds(c * 8 + p * NB + b, 1), :]
            lf[pl.ds(p * 128 + b, HD, stride=NB), :] = one[:HD]
            rf[(p * NB + b) * HD:(p * NB + b + 1) * HD, :] = one[HD:]
        lrcv[c, p * 128:(p + 1) * 128, :] = lf[p * 128:(p + 1) * 128, :].astype(BF)
        rsnd[p * 128:(p + 1) * 128, :] = rf[p * 128:(p + 1) * 128, :].astype(BF)

    def lslot(p, k):
        ref = lrcv.at[c, pl.ds(p * 128, 128)]
        return copy(ref, ref, le_s.at[p, k], le_r.at[p, k], r, wrap(c + 2 * k, NC))

    def lswap(p, k):
        ref = lrcv.at[wrap(c - 2 * k, NC), pl.ds(p * 128, 128)]
        return copy(ref, ref, lw_s.at[p, k], lw_r.at[p, k], r, cs)

    near_first = (2, 6, 4, 1, 7, 3, 5)

    place = lax.rem(c, 8)

    def rcopy(p, k):
        span = pl.ds(p * 128, 128)
        return copy(rsnd.at[span], rrcv.at[place, span], ri_s.at[p, k], ri_r.at[p, place], k, target)

    def left_send(p):
        for k in near_first:
            lslot(p, k).start()
        lswap(p, 0).start()

    def left_swap(p):
        for k in near_first:
            lslot(p, k).wait_recv()
            lswap(p, k).start()

    def right_send(p):
        for k in range(8):
            @pl.when(self_row != k)
            def _():
                rcopy(p, k).start()

    def right_wait(p):
        span = pl.ds(p * 128, 128)
        for k in range(8):
            @pl.when(jnp.logical_or(blk != r, 8 * core + k != c))
            def _():
                copy(rsnd.at[span], rrcv.at[k, span], ri_s.at[p, k], ri_r.at[p, k], r, c).wait_recv()

    col_half(0)
    left_send(0)
    right_send(0)
    col_half(1)
    left_send(1)
    right_send(1)

    @pl.when(target == c)
    def _():
        rrcv[place] = rsnd[...]

    for i in range(2):
        back_snd[:, :, i * 128:(i + 1) * 128] = upf[i].reshape(NC, 64, 128).astype(BF)

    def uc(k):
        to = wrap(c + k, NC)
        return copy(back_snd.at[to], back_rcv.at[c], u_s.at[k], u_r.at[k], r, to)

    sib_copy.wait_send()
    for g in range(G):
        zc(g).wait_send()
    for g in range(G):
        for i in range(8):
            nc(g, i).wait_send()
        for k in range(NC):
            mc(g, 1 - zl, k).wait_send()
            if k > 0:
                mc(g, zl, k).wait_send()
    for k in range(1, NR):
        lv(k).wait_send()
    for k in range(1, NC):
        lr(k).wait_send()
        lc(k).wait_send()
    for i in b_used:
        b_slot(i).wait_send()
    for i in range(1, 16):
        b_core(i // 4, i % 4).wait_send()

    left_swap(0)
    left_swap(1)
    for k in range(1, NC):
        uc(k).start()
    back_rcv[c] = back_snd[c]
    for p in range(2):
        for i in range(8):
            lswap(p, i).wait_recv()
    low4 = lax.rem(lax.broadcasted_iota(jnp.int32, (R, 128), 0), 8) < 4
    for m in range(16):
        a = lrcv[:, m * 8:(m + 1) * 8, :].astype(F32).reshape(R, 128)
        b = lrcv[:, 128 + m * 8:128 + (m + 1) * 8, :].astype(F32).reshape(R, 128)
        ltall[2 * m * R:(2 * m + 1) * R, :] = jnp.where(low4, a, pltpu.roll(b, 4, 0)).astype(BF)
        ltall[(2 * m + 1) * R:(2 * m + 2) * R, :] = jnp.where(low4, pltpu.roll(a, R - 4, 0), b).astype(BF)

    def out_copy(q):
        return pltpu.make_async_copy(
            blocks.at[lax.rem(q, 2)], pair_out.at[:, pl.ds(pl.multiple_of(q * 16, 16), 16), :], o_s.at[lax.rem(q, 2)]
        )

    def eight(q, p):
        rows = jnp.concatenate([rrcv[2 * q + t, p * 128:(p + 1) * 128, :] for t in range(2)], axis=0)
        o = dot_t(rows, ltall[...]).astype(BF)
        for j0 in range(0, 8, 2):
            two = jnp.concatenate(
                [
                    jnp.concatenate([o[j * HD:(j + 1) * HD, i * R:(i + 1) * R] for i in range(HD)], axis=0)
                    for j in (j0, j0 + 1)
                ],
                axis=1,
            )
            prod = dot(wzt[...], two)
            for i in range(2):
                j = q * 16 + (j0 + i) // NB * 8 + p * NB + (j0 + i) % NB
                one = prod[:, i * R:(i + 1) * R] * inv[pl.ds(j, 1), :]
                acc[pl.ds(j, R, stride=64), :] = one.T

    def first_half(q, carry):
        eight(q, 0)
        return carry

    def second_half(q, carry):
        eight(q, 1)

        @pl.when(q >= 2)
        def _():
            out_copy(q - 2).wait()

        for t in range(4):
            @pl.when(q == t)
            def _():
                blocks[t % 2] = acc[...].reshape(R, 64, 128)[:, t * 16:(t + 1) * 16, :].astype(BF)
        out_copy(q).start()
        return carry

    right_wait(0)
    lax.fori_loop(0, 4, first_half, 0)
    right_wait(1)
    lax.fori_loop(0, 4, second_half, 0)
    for k in range(1, NC):
        uc(k).wait_recv()
    for s in range(S):
        align[s] = jnp.concatenate([back_rcv[t, s * 8:(s + 1) * 8, :] for t in range(NC)], axis=0)
    out_copy(2).wait()
    out_copy(3).wait()

    for k in range(1, NC):
        uc(k).wait_send()
    for p in range(2):
        for k in near_first:
            lslot(p, k).wait_send()
        for i in range(8):
            lswap(p, i).wait_send()
        for k in range(8):
            @pl.when(self_row != k)
            def _():
                rcopy(p, k).wait_send()


def relay_kernel(a, b, a_out, b_out, a_mid, b_mid, sem):
    refs = [(a, a_mid, a_out, pl.ds(0, S))]
    refs += [(b, b_mid, b_out, pl.ds(i * 32, 32)) for i in range(4)]
    into = [pltpu.make_async_copy(p.at[rows], q.at[rows], sem.at[0, i]) for i, (p, q, _, rows) in enumerate(refs)]
    back = [pltpu.make_async_copy(q.at[rows], o.at[rows], sem.at[1, i]) for i, (_, q, o, rows) in enumerate(refs)]
    for cp in into:
        cp.start()
    for one, two in zip(into, back):
        one.wait()
        two.start()
    for cp in back:
        cp.wait()


def per_device(fam, pair, present, valid, wh, wo, wb, wv, wvo, wlr, wz):
    vm = pl.BlockSpec(memory_space=pltpu.VMEM)
    anywhere = pl.BlockSpec(memory_space=pl.ANY)
    dma = pltpu.SemaphoreType.DMA

    def sems(*shape):
        return [dma(shape), dma(shape)]

    scratch = [
        pltpu.VMEM((S, R, D), BF),
        pltpu.VMEM((R, 64, 128), BF),
        pltpu.VMEM((4, D, D), BF),
        pltpu.VMEM((D, D), BF),
        pltpu.VMEM((4, D, D), BF),
        pltpu.VMEM((D, D), BF),
        pltpu.VMEM((1024, 128), BF),
        pltpu.VMEM((2, 4, R, D), BF),
        pltpu.VMEM((4, 2, 4, R, D), BF),
        pltpu.VMEM((NR, S, R), F32),
        pltpu.VMEM((NC, S, R), F32),
        pltpu.VMEM((NC, S, R), F32),
        pltpu.VMEM((512, 128), F32),
        pltpu.VMEM((H, 64, 128), BF),
        pltpu.VMEM((H, 64, 128), BF),
        pltpu.VMEM((2, NR, H, R, 128), BF),
        pltpu.VMEM((4, 2 * R, D), BF),
        pltpu.VMEM((4, 2 * R, D), F32),
        pltpu.VMEM((4, NR * R, D), BF),
        pltpu.VMEM((4, NR * R, D), BF),
        pltpu.VMEM((2, 2, R, D), F32),
        pltpu.VMEM((NB * R, D), BF),
        pltpu.VMEM((NB * R, D), BF),
        pltpu.VMEM((NB * R, D), BF),
        pltpu.VMEM((NB * R, D), F32),
        pltpu.VMEM((NB * R, D), BF),
        pltpu.VMEM((2, NC, 32, D), BF),
        pltpu.VMEM((NC, 2, 32, D), BF),
        pltpu.VMEM((2, 1024, 128), F32),
        pltpu.VMEM((2, 1024, 128), F32),
        pltpu.VMEM((2, 1024, 128), F32),
        pltpu.VMEM((NC, 64, D), BF),
        pltpu.VMEM((NC, 64, D), BF),
        pltpu.VMEM((256, 128), F32),
        pltpu.VMEM((256, 128), F32),
        pltpu.VMEM((NC, 256, 128), BF),
        pltpu.VMEM((256, 128), BF),
        pltpu.VMEM((8, 256, 128), BF),
        pltpu.VMEM((R, 128), F32),
        pltpu.VMEM((R, 128), F32),
        pltpu.VMEM((64, 128), F32),
        pltpu.VMEM((HD * R, 128), BF),
        pltpu.VMEM((128, 1024), BF),
        pltpu.VMEM((R * 64, 128), F32),
        pltpu.VMEM((2, R, 16, 128), BF),
        *sems(G), *sems(G, 8), *sems(8), *sems(16), *sems(16), dma, dma, *sems(20), *sems(15),
        *sems(G, 2, 16), *sems(16), *sems(2, 8), *sems(2, 8), *sems(2, 8), dma((2,)), dma((7,)),
    ]
    align, pair_out = pl.pallas_call(
        msa_kernel,
        out_shape=(jax.ShapeDtypeStruct((S, R, D), BF), jax.ShapeDtypeStruct((R, 64, 128), BF)),
        in_specs=[anywhere, anywhere, vm, vm, anywhere, anywhere, vm, anywhere, anywhere, vm, anywhere],
        out_specs=(vm, pl.BlockSpec(memory_space=pl.ANY)),
        scratch_shapes=scratch,
        compiler_params=pltpu.CompilerParams(
            has_side_effects=True, collective_id=0, vmem_limit_bytes=60 * 1024 * 1024
        ),
        name="msa",
    )(
        fam, pair, present, valid.reshape(NR, R), wh, wo, wb.T, wv, wvo,
        wlr.transpose(0, 2, 1).reshape(64, D), wz,
    )
    return pl.pallas_call(
        relay_kernel,
        out_shape=(jax.ShapeDtypeStruct((S, R, D), BF), jax.ShapeDtypeStruct((R, 64, 128), BF)),
        in_specs=[anywhere] * 2,
        out_specs=(anywhere,) * 2,
        scratch_shapes=[pltpu.VMEM((S, R, D), BF), pltpu.VMEM((R, 64, 128), BF), dma((2, 5))],
        compiler_params=pltpu.CompilerParams(vmem_limit_bytes=60 * 1024 * 1024),
        name="relay",
    )(align, pair_out)


def solution(mesh):
    in_specs = (P("col", "row", None), P("row", "col", None), P("col", "row")) + (P(),) * 8
    out_specs = (P("col", "row", None), P("row", "col", None))
    return jax.shard_map(per_device, mesh=mesh, in_specs=in_specs, out_specs=out_specs, check_vma=False)
```

```python
import jax
import jax.numpy as jnp
from jax import lax
from jax.experimental import pallas as pl
from jax.experimental.pallas import tpu as pltpu
from jax.sharding import PartitionSpec as P

BF = jnp.bfloat16
F32 = jnp.float32
EPS = 1e-05
MASK_BIG = 1000000000.0
MESH = pl.DeviceIdType.MESH

NR = 8
NC = 16
S = 8
R = 128
D = 256
H = 8
HD = 32
G = 2
NB = 4


def norm(x):
    c = x - jnp.mean(x, axis=-1, keepdims=True)
    return c * lax.rsqrt(jnp.mean(c * c, axis=-1, keepdims=True) + EPS)


def dot(a, b):
    return jnp.dot(a, b, preferred_element_type=F32)


def dot_t(a, b):
    return lax.dot_general(a, b, (((1,), (1,)), ((), ())), preferred_element_type=F32)


def sigmoid(x):
    return 1.0 / (1.0 + jnp.exp(-x))


def head_lanes(rows):
    return lax.broadcasted_iota(jnp.int32, (rows, D), 1) // HD


def attend(q, k, v, score_of, step):
    n = q.shape[0]
    lanes = head_lanes(n)
    total = jnp.zeros((n, D), F32)
    for h0 in range(0, H, step):
        heads = range(h0, h0 + step)
        stacked = jnp.concatenate([jnp.where(lanes == h, q, jnp.zeros_like(q)) for h in heads], axis=0)
        raw = dot_t(stacked, k)
        parts, sums = [], []
        for at, h in enumerate(heads):
            s = score_of(h, raw[at * n:(at + 1) * n])
            p = jnp.exp(s - jnp.max(s, axis=-1, keepdims=True))
            sums.append(jnp.sum(p, axis=-1, keepdims=True))
            parts.append(p.astype(BF))
        out = dot(jnp.concatenate(parts, axis=0), v)
        for at, h in enumerate(heads):
            total = jnp.where(lanes == h, out[at * n:(at + 1) * n] * (1.0 / sums[at]), total)
    return total


def msa_kernel(
    fam_in, pair_in, present, valid, wh_in, wo_in, wb, wv_in, wvo_in, wlr, wz_in,
    align, pair_out,
    fam, pair, wh, wo, wv, wvo, wz, ft, nall, livr, lres, lcol, bscr, mine, sib, ball, qs, gs, ks, vs, midf, cqs, cks, cvs, cgs, cos, snd, rcv,
    xf, nf, upf, back_snd, back_rcv, lf, rf, lrcv, rsnd, rrcv, ltt, cmask, inv, ltall, wzt, acc, blocks,
    z_s, z_r, n_s, n_r, lv_s, lv_r, lr_s, lr_r, lc_s, lc_r, sb_s, sb_r, b_s, b_r, bc_s, bc_r,
    m_s, m_r, u_s, u_r, le_s, le_r, lw_s, lw_r, ri_s, ri_r, o_s, in_s,
):
    r = lax.axis_index("row")
    c = lax.axis_index("col")
    core = lax.rem(c, 2)
    blk = c // 2
    x, zl = r // 2, lax.rem(r, 2)
    y, zh = c // 4, lax.rem(blk, 2)
    z = zh * 2 + zl
    rz = 2 * x + 1 - zl
    cs = c + 1 - 2 * core
    target = 2 * r + c // 8
    self_row = jnp.where(target == c, r, -1)

    pairs = [(fam_in, fam), (pair_in, pair), (wh_in, wh), (wo_in, wo), (wv_in, wv), (wvo_in, wvo), (wz_in, wz)]
    loads = [pltpu.make_async_copy(a, b, in_s.at[i]) for i, (a, b) in enumerate(pairs)]
    for cp in loads:
        cp.start()

    def wrap(i, n):
        return lax.rem(i + n, n)

    def copy(src, dst, ss, rs, row, col):
        return pltpu.make_async_remote_copy(
            src_ref=src, dst_ref=dst, send_sem=ss, recv_sem=rs, device_id=(row, col), device_id_type=MESH
        )

    barrier = pltpu.get_barrier_semaphore()

    def greet(row, col):
        pl.semaphore_signal(barrier, inc=1, device_id=(row, col), device_id_type=MESH)

    for k in range(1, NR):
        greet(wrap(r + k, NR), c)
    for k in range(1, NC):
        greet(r, wrap(c + k, NC))
        greet(rz, wrap(c + k, NC))
    for k in range(8):
        @pl.when(self_row != k)
        def _():
            greet(k, target)

        @pl.when(jnp.logical_or(blk != r, 8 * core + k != c))
        def _():
            greet(blk, 8 * core + k)

    def zc(g):
        src = fam.at[pl.ds(4 * (1 - zl) + 2 * g, 2)]
        return copy(src, ft.at[zl, pl.ds(2 * g, 2)], z_s.at[g], z_r.at[g], rz, c)

    xl, xr = wrap(x + 3, 4), wrap(x + 1, 4)
    n_plan = [
        (x, zl, 0, 2, xr), (x, zl, 0, 2, xl), (x, 1 - zl, 0, 2, xr), (x, 1 - zl, 0, 2, xl),
        (xl, zl, 0, 1, xr), (xr, zl, 1, 1, xl), (xl, 1 - zl, 0, 1, xr), (xr, 1 - zl, 1, 1, xl),
    ]

    def nc(g, i):
        xb, zb, lo, n, to = n_plan[i]
        ref = nall.at[xb, zb, pl.ds(2 * g + lo, n)]
        return copy(ref, ref, n_s.at[g, i], n_r.at[g, i], 2 * to + zl, c)

    first = core == 0
    h0 = core * 4

    def at(dp, dq):
        by = wrap(y + jnp.where(first, dq, dp), 4)
        bz = wrap(z + jnp.where(first, dp, dq), 4)
        return by, bz

    def bref(dp, dq, lo, n):
        by, bz = at(dp, dq)
        return ball.at[lax.rem(bz, 2), by * 2 + bz // 2, pl.ds(h0 + lo, n)]

    def bc(slot, dp, dq, lo, n, to_p, to_q):
        ty, tz = at(to_p, to_q)
        ref = bref(dp, dq, lo, n)
        return copy(ref, ref, b_s.at[slot], b_r.at[slot], 2 * x + lax.rem(tz, 2), 4 * ty + 2 * (tz // 2) + core)

    in_pair, out_pair = 1 + 2 * zl, 3 - 2 * zl
    along = (0, 3, 1, 2)

    def b_slot(i):
        if i == 0:
            return bc(0, 0, 0, 0, 4, 1, 0)
        if i == 1:
            return bc(1, 0, 0, 0, 4, 3, 0)
        if i == 2:
            return bc(2, 0, 0, 0, 4, 2, 0)
        if i == 3:
            return bc(3, 2, 0, 0, 4, 0, 2)
        dp = along[(i - 4) % 4]
        if i < 8:
            return bc(i, dp, 0, 0, 4, 0, 1)
        if i < 12:
            return bc(i, dp, 0, 0, 4, 0, 3)
        if i < 15:
            return bc(i, dp, jnp.where(first, 3, in_pair), 0, 2, 0, jnp.where(first, 1, out_pair))
        return bc(i, dp, jnp.where(first, 1, in_pair), 2, 2, 0, jnp.where(first, 3, out_pair))

    b_used = [i for i in range(19) if i != 15]

    def b_core(dp, dq):
        ref = bref(dp, dq, 0, 4)
        i = dp * 4 + dq - 1
        return copy(ref, ref, bc_s.at[i], bc_r.at[i], r, cs)

    def b_start(*slots):
        for i in slots:
            b_slot(i).start()

    def b_wait(*slots):
        for i in slots:
            b_slot(i).wait_recv()

    def b_swap(*pairs):
        for p in pairs:
            b_core(*p).start()

    livr[r] = (present[...] * valid[pl.ds(r, 1), :]).astype(F32)
    loads[0].wait()
    ft[zl] = fam[pl.ds(4 * zl, 4)]
    pl.semaphore_wait(barrier, jnp.where(target == c, 51, 53))
    for g in range(G):
        zc(g).start()
    for g in range(G):
        for s in (2 * g, 2 * g + 1):
            nall[x, zl, s] = norm(ft[zl, s].astype(F32)).astype(BF)
        for i in (0, 1):
            nc(g, i).start()

    def lv(k):
        return copy(livr.at[r], livr.at[r], lv_s.at[k], lv_r.at[k], wrap(r + k, NR), c)

    for k in range(1, NR):
        lv(k).start()

    def bias_step(t, carry):
        lo = pair[pl.ds(t * 8, 8)]
        hi = pair[pl.ds(64 + t * 8, 8)]
        both = jnp.concatenate([lo, hi], axis=1).reshape(1024, 128)
        off = both.astype(F32) - dot(both, jnp.full((128, 128), 1 / 128, BF))
        rows = (off * lax.rsqrt(jnp.mean(off * off, axis=-1, keepdims=True) + EPS)).astype(BF)
        b = dot_t(wb[...], rows)
        for i in range(8):
            bscr[pl.ds(t * 64 + i * 8, 8), :] = b[:, i * 128:(i + 1) * 128]
        return carry

    loads[1].wait()
    lax.fori_loop(0, 8, bias_step, 0, unroll=8)
    for h in range(H):
        mine[h] = bscr[pl.ds(h, 64, stride=8), :].astype(BF)
    sib_copy = copy(mine, sib, sb_s, sb_r, r, cs)
    sib_copy.start()

    def pass_on(g, i):
        for k in (i, i + 1):
            nc(g, k).wait_recv()
        for k in (i + 4, i + 5):
            nc(g, k).start()

    def partner(g):
        zc(g).wait_recv()
        for s in (2 * g, 2 * g + 1):
            nall[x, 1 - zl, s] = norm(ft[1 - zl, s].astype(F32)).astype(BF)
        for i in (2, 3):
            nc(g, i).start()

    def query(zb, s):
        rows = nall[x, zb, s]
        qs[s, pl.ds(pl.multiple_of(zb * R, R), R), :] = (dot(rows, wh[0]) * (HD ** -0.5)).astype(BF)
        gs[s, pl.ds(pl.multiple_of(zb * R, R), R), :] = sigmoid(dot(rows, wh[3]))

    sib_copy.wait_recv()
    low = lax.broadcasted_iota(jnp.int32, (64, 128), 1) < 64
    for h in range(H):
        a = mine[h].astype(F32)
        b = sib[h].astype(F32)
        left_part = jnp.where(first, a, b)
        right_part = jnp.where(first, b, a)
        ball[zl, blk, h, 0:64, :] = jnp.where(low, left_part, pltpu.roll(right_part, 64, 1)).astype(BF)
        ball[zl, blk, h, 64:128, :] = jnp.where(low, pltpu.roll(left_part, 64, 1), right_part).astype(BF)
    b_start(0, 1, 2, 4, 8)
    partner(0)
    partner(1)
    loads[2].wait()
    query(zl, 0)
    pass_on(0, 0)
    b_wait(0, 1)
    b_start(5, 9, 6, 10)
    b_swap((3, 0), (1, 0))
    b_wait(2)
    b_start(7, 11, 3)
    b_swap((2, 0))
    query(zl, 1)
    b_wait(4, 8)
    b_start(12, 16)
    b_swap((0, 3), (0, 1))
    pass_on(0, 2)
    query(zl, 2)
    pass_on(1, 0)
    query(zl, 3)
    b_wait(5, 9)
    b_start(13, 17)
    b_swap((3, 3), (3, 1))
    query(1 - zl, 0)
    b_wait(6, 10)
    b_start(14, 18)
    b_swap((1, 3), (1, 1))
    pass_on(1, 2)

    for k in range(1, NR):
        lv(k).wait_recv()
    lres[c] = livr[r]
    lcol[c] = livr[blk]

    def lr(k):
        return copy(livr.at[r], lres.at[c], lr_s.at[k], lr_r.at[k], r, wrap(c + k, NC))

    def lc(k):
        to = wrap(c + k, NC)
        return copy(livr.at[to // 2], lcol.at[c], lc_s.at[k], lc_r.at[k], r, to)

    for k in range(1, NC):
        lr(k).start()
        lc(k).start()

    for s in (1, 2, 3):
        query(1 - zl, s)
    b_wait(12, 16)
    b_swap((0, 2))
    b_wait(7, 11)
    b_swap((2, 3), (2, 1))

    def keys_values(g):
        for i in (4, 5, 6, 7):
            nc(g, i).wait_recv()
        for s in (2 * g, 2 * g + 1):
            for b in range(NR):
                rows = nall[b // 2, b % 2, s]
                ks[s, b * R:(b + 1) * R, :] = dot(rows, wh[1]).astype(BF)
                vs[s, b * R:(b + 1) * R, :] = dot(rows, wh[2]).astype(BF)

    keys_values(0)
    b_wait(13, 17)
    b_swap((3, 2))
    b_wait(14, 18)
    b_swap((1, 2))
    b_wait(3)
    b_swap((2, 2))
    loads[3].wait()
    for i in range(1, 16):
        b_core(i // 4, i % 4).wait_recv()

    def mc(g, zb, k):
        to = wrap(c + k, NC)
        return copy(
            snd.at[zb, to, pl.ds(g * 16, 16)], rcv.at[c, zl, pl.ds(g * 16, 16)],
            m_s.at[g, jnp.where(zb == zl, 0, 1), k], m_r.at[g, jnp.where(zb == zl, 0, 1), k],
            2 * x + zb, to,
        )

    def group(g):
        def row_one(i, carry):
            s = 2 * g + i
            keep = jnp.concatenate([livr[b, pl.ds(4 * zl + s, 1), :] for b in range(NR)], axis=1) > 0.5

            def score(h, raw):
                bias = jnp.concatenate(
                    [jnp.concatenate([ball[zb, b, h] for b in range(NR)], axis=1) for zb in range(2)], axis=0
                )
                return jnp.where(keep, raw + bias.astype(F32), -MASK_BIG)

            o = attend(qs[s], ks[s], vs[s], score, 1)
            delta = dot((gs[s] * o).astype(BF), wo[...])
            for zb in range(2):
                midf[i, zb] = ft[zb, s].astype(F32) + delta[zb * R:(zb + 1) * R]
            return carry

        lax.fori_loop(0, 2, row_one, 0)
        for zb in range(2):
            for t in range(NC):
                two = jnp.concatenate([midf[i, zb, t * 8:(t + 1) * 8, :] for i in range(2)], axis=0)
                snd[zb, t, g * 16:(g + 1) * 16, :] = two.astype(BF)
        for k in range(NC):
            mc(g, 1 - zl, k).start()
            if k > 0:
                mc(g, zl, k).start()

    group(0)
    keys_values(1)
    group(1)
    rcv[c, zl] = snd[zl, c]

    for k in range(1, NC):
        lr(k).wait_recv()
        lc(k).wait_recv()
    by_res = lres[...].reshape(R, R).T
    cmask[...] = by_res
    ltt[...] = lcol[...].reshape(R, R).T
    right_live = ltt[pl.ds(pl.multiple_of(core * 64, 64), 64), :]
    inv[...] = 1.0 / jnp.maximum(dot_t(right_live.astype(BF), by_res.astype(BF)), 1.0)
    for i in (4, 5, 6):
        loads[i].wait()
    wzt[...] = wz[...].astype(F32).T.astype(BF)
    for g in range(G):
        for k in range(NC):
            mc(g, 1 - zl, k).wait_recv()
            if k > 0:
                mc(g, zl, k).wait_recv()
        for t in range(0, NC, 4):
            mid = rcv[t:t + 4, :, g * 16:(g + 1) * 16, :].reshape(128, D).astype(F32)
            normed = norm(mid)
            for u in range(8):
                to = slice(t * 64 + u * 32 + g * 16, t * 64 + u * 32 + g * 16 + 16)
                for i in range(2):
                    xf[i, to, :] = mid[u * 16:(u + 1) * 16, i * 128:(i + 1) * 128]
                    nf[i, to, :] = normed[u * 16:(u + 1) * 16, i * 128:(i + 1) * 128]

    def rows_of(ref, p):
        return jnp.concatenate(
            [
                jnp.concatenate([ref[i, pl.ds(p * NB + b, R, stride=8), :] for i in range(2)], axis=1)
                for b in range(NB)
            ],
            axis=0,
        )

    def col_half(p):
        rows = rows_of(nf, p).astype(BF)
        cqs[...] = (dot(rows, wv[0]) * (HD ** -0.5)).astype(BF)
        cks[...] = dot(rows, wv[1]).astype(BF)
        cvs[...] = dot(rows, wv[2]).astype(BF)
        cgs[...] = sigmoid(dot(rows, wv[3]))
        for b in range(NB):
            row = cmask[pl.ds(c * 8 + p * NB + b, 1), :]
            span = slice(b * R, (b + 1) * R)

            def score(h, raw):
                return jnp.where(row > 0.5, raw, -MASK_BIG)

            o = attend(cqs[span, :], cks[span, :], cvs[span, :], score, 2)
            cos[span, :] = (cgs[span, :] * o).astype(BF)
        up = (rows_of(xf, p) + dot(cos[...], wvo[...])).astype(BF).astype(F32)
        both = dot_t(wlr[...], norm(up).astype(BF))
        for b in range(NB):
            span = slice(b * R, (b + 1) * R)
            for i in range(2):
                upf[i, pl.ds(p * NB + b, R, stride=8), :] = up[span, i * 128:(i + 1) * 128]
            one = both[:, span] * cmask[pl.ds(c * 8 + p * NB + b, 1), :]
            lf[pl.ds(p * 128 + b, HD, stride=NB), :] = one[:HD]
            rf[(p * NB + b) * HD:(p * NB + b + 1) * HD, :] = one[HD:]
        lrcv[c, p * 128:(p + 1) * 128, :] = lf[p * 128:(p + 1) * 128, :].astype(BF)
        rsnd[p * 128:(p + 1) * 128, :] = rf[p * 128:(p + 1) * 128, :].astype(BF)

    def lslot(p, k):
        ref = lrcv.at[c, pl.ds(p * 128, 128)]
        return copy(ref, ref, le_s.at[p, k], le_r.at[p, k], r, wrap(c + 2 * k, NC))

    def lswap(p, k):
        ref = lrcv.at[wrap(c - 2 * k, NC), pl.ds(p * 128, 128)]
        return copy(ref, ref, lw_s.at[p, k], lw_r.at[p, k], r, cs)

    near_first = (2, 6, 4, 1, 7, 3, 5)

    place = lax.rem(c, 8)

    def rcopy(p, k):
        span = pl.ds(p * 128, 128)
        return copy(rsnd.at[span], rrcv.at[place, span], ri_s.at[p, k], ri_r.at[p, place], k, target)

    def left_send(p):
        for k in near_first:
            lslot(p, k).start()
        lswap(p, 0).start()

    def left_swap(p):
        for k in near_first:
            lslot(p, k).wait_recv()
            lswap(p, k).start()

    def right_send(p):
        for k in range(8):
            @pl.when(self_row != k)
            def _():
                rcopy(p, k).start()

    def right_wait(p):
        span = pl.ds(p * 128, 128)
        for k in range(8):
            @pl.when(jnp.logical_or(blk != r, 8 * core + k != c))
            def _():
                copy(rsnd.at[span], rrcv.at[k, span], ri_s.at[p, k], ri_r.at[p, k], r, c).wait_recv()

    col_half(0)
    left_send(0)
    right_send(0)
    col_half(1)
    left_send(1)

    @pl.when(target == c)
    def _():
        rrcv[place] = rsnd[...]

    for i in range(2):
        back_snd[:, :, i * 128:(i + 1) * 128] = upf[i].reshape(NC, 64, 128).astype(BF)

    def uc(k):
        to = wrap(c + k, NC)
        return copy(back_snd.at[to], back_rcv.at[c], u_s.at[k], u_r.at[k], r, to)

    sib_copy.wait_send()
    for g in range(G):
        zc(g).wait_send()
    for g in range(G):
        for i in range(8):
            nc(g, i).wait_send()
        for k in range(NC):
            mc(g, 1 - zl, k).wait_send()
            if k > 0:
                mc(g, zl, k).wait_send()
    for k in range(1, NR):
        lv(k).wait_send()
    for k in range(1, NC):
        lr(k).wait_send()
        lc(k).wait_send()
    for i in b_used:
        b_slot(i).wait_send()
    for i in range(1, 16):
        b_core(i // 4, i % 4).wait_send()

    left_swap(0)
    right_send(1)
    left_swap(1)
    for k in range(1, NC):
        uc(k).start()
    back_rcv[c] = back_snd[c]
    for p in range(2):
        for i in range(8):
            lswap(p, i).wait_recv()
    low4 = lax.rem(lax.broadcasted_iota(jnp.int32, (R, 128), 0), 8) < 4
    for m in range(16):
        a = lrcv[:, m * 8:(m + 1) * 8, :].astype(F32).reshape(R, 128)
        b = lrcv[:, 128 + m * 8:128 + (m + 1) * 8, :].astype(F32).reshape(R, 128)
        ltall[2 * m * R:(2 * m + 1) * R, :] = jnp.where(low4, a, pltpu.roll(b, 4, 0)).astype(BF)
        ltall[(2 * m + 1) * R:(2 * m + 2) * R, :] = jnp.where(low4, pltpu.roll(a, R - 4, 0), b).astype(BF)

    def out_copy(q):
        return pltpu.make_async_copy(blocks.at[q], pair_out.at[:, pl.ds(q * 16, 16), :], o_s.at[q])

    def sixteen(q, p):
        rows = jnp.concatenate([rrcv[4 * q + t, p * 128:(p + 1) * 128, :] for t in range(4)], axis=0)
        o = dot_t(rows, ltall[...]).astype(BF)
        for j0 in range(0, 16, 2):
            two = jnp.concatenate(
                [
                    jnp.concatenate([o[j * HD:(j + 1) * HD, i * R:(i + 1) * R] for i in range(HD)], axis=0)
                    for j in (j0, j0 + 1)
                ],
                axis=1,
            )
            prod = dot(wzt[...], two)
            for i in range(2):
                j = q * 32 + (j0 + i) // NB * 8 + p * NB + (j0 + i) % NB
                one = prod[:, i * R:(i + 1) * R] * inv[pl.ds(j, 1), :]
                acc[pl.ds(j, R, stride=64), :] = one.T

    def first_half(q, carry):
        sixteen(q, 0)
        return carry

    right_wait(0)
    lax.fori_loop(0, 2, first_half, 0)
    right_wait(1)
    for q in range(2):
        sixteen(q, 1)
        for t in (2 * q, 2 * q + 1):
            blocks[t] = acc[...].reshape(R, 64, 128)[:, t * 16:(t + 1) * 16, :].astype(BF)
            out_copy(t).start()
    for k in range(1, NC):
        uc(k).wait_recv()
    for s in range(S):
        align[s] = jnp.concatenate([back_rcv[t, s * 8:(s + 1) * 8, :] for t in range(NC)], axis=0)
    for q in range(4):
        out_copy(q).wait()

    for k in range(1, NC):
        uc(k).wait_send()
    for p in range(2):
        for k in near_first:
            lslot(p, k).wait_send()
        for i in range(8):
            lswap(p, i).wait_send()
        for k in range(8):
            @pl.when(self_row != k)
            def _():
                rcopy(p, k).wait_send()


def relay_kernel(a, b, a_out, b_out, a_mid, b_mid, sem):
    refs = [(a, a_mid, a_out, pl.ds(0, S))]
    refs += [(b, b_mid, b_out, pl.ds(i * 32, 32)) for i in range(4)]
    into = [pltpu.make_async_copy(p.at[rows], q.at[rows], sem.at[0, i]) for i, (p, q, _, rows) in enumerate(refs)]
    back = [pltpu.make_async_copy(q.at[rows], o.at[rows], sem.at[1, i]) for i, (_, q, o, rows) in enumerate(refs)]
    for cp in into:
        cp.start()
    for one, two in zip(into, back):
        one.wait()
        two.start()
    for cp in back:
        cp.wait()


def per_device(fam, pair, present, valid, wh, wo, wb, wv, wvo, wlr, wz):
    vm = pl.BlockSpec(memory_space=pltpu.VMEM)
    anywhere = pl.BlockSpec(memory_space=pl.ANY)
    dma = pltpu.SemaphoreType.DMA

    def sems(*shape):
        return [dma(shape), dma(shape)]

    scratch = [
        pltpu.VMEM((S, R, D), BF),
        pltpu.VMEM((R, 64, 128), BF),
        pltpu.VMEM((4, D, D), BF),
        pltpu.VMEM((D, D), BF),
        pltpu.VMEM((4, D, D), BF),
        pltpu.VMEM((D, D), BF),
        pltpu.VMEM((1024, 128), BF),
        pltpu.VMEM((2, 4, R, D), BF),
        pltpu.VMEM((4, 2, 4, R, D), BF),
        pltpu.VMEM((NR, S, R), F32),
        pltpu.VMEM((NC, S, R), F32),
        pltpu.VMEM((NC, S, R), F32),
        pltpu.VMEM((512, 128), F32),
        pltpu.VMEM((H, 64, 128), BF),
        pltpu.VMEM((H, 64, 128), BF),
        pltpu.VMEM((2, NR, H, R, 128), BF),
        pltpu.VMEM((4, 2 * R, D), BF),
        pltpu.VMEM((4, 2 * R, D), F32),
        pltpu.VMEM((4, NR * R, D), BF),
        pltpu.VMEM((4, NR * R, D), BF),
        pltpu.VMEM((2, 2, R, D), F32),
        pltpu.VMEM((NB * R, D), BF),
        pltpu.VMEM((NB * R, D), BF),
        pltpu.VMEM((NB * R, D), BF),
        pltpu.VMEM((NB * R, D), F32),
        pltpu.VMEM((NB * R, D), BF),
        pltpu.VMEM((2, NC, 32, D), BF),
        pltpu.VMEM((NC, 2, 32, D), BF),
        pltpu.VMEM((2, 1024, 128), F32),
        pltpu.VMEM((2, 1024, 128), F32),
        pltpu.VMEM((2, 1024, 128), F32),
        pltpu.VMEM((NC, 64, D), BF),
        pltpu.VMEM((NC, 64, D), BF),
        pltpu.VMEM((256, 128), F32),
        pltpu.VMEM((256, 128), F32),
        pltpu.VMEM((NC, 256, 128), BF),
        pltpu.VMEM((256, 128), BF),
        pltpu.VMEM((8, 256, 128), BF),
        pltpu.VMEM((R, 128), F32),
        pltpu.VMEM((R, 128), F32),
        pltpu.VMEM((64, 128), F32),
        pltpu.VMEM((HD * R, 128), BF),
        pltpu.VMEM((128, 1024), BF),
        pltpu.VMEM((R * 64, 128), F32),
        pltpu.VMEM((4, R, 16, 128), BF),
        *sems(G), *sems(G, 8), *sems(8), *sems(16), *sems(16), dma, dma, *sems(20), *sems(15),
        *sems(G, 2, 16), *sems(16), *sems(2, 8), *sems(2, 8), *sems(2, 8), dma((4,)), dma((7,)),
    ]
    align, pair_out = pl.pallas_call(
        msa_kernel,
        out_shape=(jax.ShapeDtypeStruct((S, R, D), BF), jax.ShapeDtypeStruct((R, 64, 128), BF)),
        in_specs=[anywhere, anywhere, vm, vm, anywhere, anywhere, vm, anywhere, anywhere, vm, anywhere],
        out_specs=(vm, pl.BlockSpec(memory_space=pl.ANY)),
        scratch_shapes=scratch,
        compiler_params=pltpu.CompilerParams(
            has_side_effects=True, collective_id=0, vmem_limit_bytes=60 * 1024 * 1024
        ),
        name="msa",
    )(
        fam, pair, present, valid.reshape(NR, R), wh, wo, wb.T, wv, wvo,
        wlr.transpose(0, 2, 1).reshape(64, D), wz,
    )
    return pl.pallas_call(
        relay_kernel,
        out_shape=(jax.ShapeDtypeStruct((S, R, D), BF), jax.ShapeDtypeStruct((R, 64, 128), BF)),
        in_specs=[anywhere] * 2,
        out_specs=(anywhere,) * 2,
        scratch_shapes=[pltpu.VMEM((S, R, D), BF), pltpu.VMEM((R, 64, 128), BF), dma((2, 5))],
        compiler_params=pltpu.CompilerParams(vmem_limit_bytes=60 * 1024 * 1024),
        name="relay",
    )(align, pair_out)


def solution(mesh):
    in_specs = (P("col", "row", None), P("row", "col", None), P("col", "row")) + (P(),) * 8
    out_specs = (P("col", "row", None), P("row", "col", None))
    return jax.shard_map(per_device, mesh=mesh, in_specs=in_specs, out_specs=out_specs, check_vma=False)
```

```python
import jax
import jax.numpy as jnp
from jax import lax
from jax.experimental import pallas as pl
from jax.experimental.pallas import tpu as pltpu
from jax.sharding import PartitionSpec as P

BF = jnp.bfloat16
F32 = jnp.float32
EPS = 1e-05
MASK_BIG = 1000000000.0
MESH = pl.DeviceIdType.MESH

NR = 8
NC = 16
S = 8
R = 128
D = 256
H = 8
HD = 32
G = 2
NB = 4


def norm(x):
    c = x - jnp.mean(x, axis=-1, keepdims=True)
    return c * lax.rsqrt(jnp.mean(c * c, axis=-1, keepdims=True) + EPS)


def dot(a, b):
    return jnp.dot(a, b, preferred_element_type=F32)


def dot_t(a, b):
    return lax.dot_general(a, b, (((1,), (1,)), ((), ())), preferred_element_type=F32)


def sigmoid(x):
    return 1.0 / (1.0 + jnp.exp(-x))


def head_lanes(rows):
    return lax.broadcasted_iota(jnp.int32, (rows, D), 1) // HD


def attend(q, k, v, score_of, step):
    n = q.shape[0]
    lanes = head_lanes(n)
    total = jnp.zeros((n, D), F32)
    for h0 in range(0, H, step):
        heads = range(h0, h0 + step)
        stacked = jnp.concatenate([jnp.where(lanes == h, q, jnp.zeros_like(q)) for h in heads], axis=0)
        raw = dot_t(stacked, k)
        parts, sums = [], []
        for at, h in enumerate(heads):
            s = score_of(h, raw[at * n:(at + 1) * n])
            p = jnp.exp(s - jnp.max(s, axis=-1, keepdims=True))
            sums.append(jnp.sum(p, axis=-1, keepdims=True))
            parts.append(p.astype(BF))
        out = dot(jnp.concatenate(parts, axis=0), v)
        for at, h in enumerate(heads):
            total = jnp.where(lanes == h, out[at * n:(at + 1) * n] * (1.0 / sums[at]), total)
    return total


def msa_kernel(
    fam_in, pair_in, present, valid, wh_in, wo_in, wb, wv_in, wvo_in, wlr, wz_in,
    align, pair_out,
    fam, pair, wh, wo, wv, wvo, wz, ft, nall, livr, lres, lcol, bscr, mine, sib, ball, qs, gs, ks, vs, midf, cqs, cks, cvs, cgs, cos, snd, rcv,
    xf, nf, upf, back_snd, back_rcv, lf, rf, lrcv, rsnd, rrcv, ltt, cmask, inv, ltall, wzt, acc, blocks,
    z_s, z_r, n_s, n_r, lv_s, lv_r, lr_s, lr_r, lc_s, lc_r, sb_s, sb_r, b_s, b_r, bc_s, bc_r,
    m_s, m_r, u_s, u_r, le_s, le_r, lw_s, lw_r, ri_s, ri_r, o_s, in_s,
):
    r = lax.axis_index("row")
    c = lax.axis_index("col")
    core = lax.rem(c, 2)
    blk = c // 2
    x, zl = r // 2, lax.rem(r, 2)
    y, zh = c // 4, lax.rem(blk, 2)
    z = zh * 2 + zl
    rz = 2 * x + 1 - zl
    cs = c + 1 - 2 * core
    target = 2 * r + c // 8
    self_row = jnp.where(target == c, r, -1)

    pairs = [(fam_in, fam), (pair_in, pair), (wh_in, wh), (wo_in, wo), (wv_in, wv), (wvo_in, wvo), (wz_in, wz)]
    loads = [pltpu.make_async_copy(a, b, in_s.at[i]) for i, (a, b) in enumerate(pairs)]
    for cp in loads:
        cp.start()

    def wrap(i, n):
        return lax.rem(i + n, n)

    def copy(src, dst, ss, rs, row, col):
        return pltpu.make_async_remote_copy(
            src_ref=src, dst_ref=dst, send_sem=ss, recv_sem=rs, device_id=(row, col), device_id_type=MESH
        )

    barrier = pltpu.get_barrier_semaphore()

    def greet(row, col):
        pl.semaphore_signal(barrier, inc=1, device_id=(row, col), device_id_type=MESH)

    for k in range(1, NR):
        greet(wrap(r + k, NR), c)
    for k in range(1, NC):
        greet(r, wrap(c + k, NC))
        greet(rz, wrap(c + k, NC))
    for k in range(8):
        @pl.when(self_row != k)
        def _():
            greet(k, target)

        @pl.when(jnp.logical_or(blk != r, 8 * core + k != c))
        def _():
            greet(blk, 8 * core + k)

    def zc(g):
        src = fam.at[pl.ds(4 * (1 - zl) + 2 * g, 2)]
        return copy(src, ft.at[zl, pl.ds(2 * g, 2)], z_s.at[g], z_r.at[g], rz, c)

    xl, xr = wrap(x + 3, 4), wrap(x + 1, 4)
    n_plan = [
        (x, zl, 0, 2, xr), (x, zl, 0, 2, xl), (x, 1 - zl, 0, 2, xr), (x, 1 - zl, 0, 2, xl),
        (xl, zl, 0, 1, xr), (xr, zl, 1, 1, xl), (xl, 1 - zl, 0, 1, xr), (xr, 1 - zl, 1, 1, xl),
    ]

    def nc(g, i):
        xb, zb, lo, n, to = n_plan[i]
        ref = nall.at[xb, zb, pl.ds(2 * g + lo, n)]
        return copy(ref, ref, n_s.at[g, i], n_r.at[g, i], 2 * to + zl, c)

    first = core == 0
    h0 = core * 4

    def at(dp, dq):
        by = wrap(y + jnp.where(first, dq, dp), 4)
        bz = wrap(z + jnp.where(first, dp, dq), 4)
        return by, bz

    def bref(dp, dq, lo, n):
        by, bz = at(dp, dq)
        return ball.at[lax.rem(bz, 2), by * 2 + bz // 2, pl.ds(h0 + lo, n)]

    def bc(slot, dp, dq, lo, n, to_p, to_q):
        ty, tz = at(to_p, to_q)
        ref = bref(dp, dq, lo, n)
        return copy(ref, ref, b_s.at[slot], b_r.at[slot], 2 * x + lax.rem(tz, 2), 4 * ty + 2 * (tz // 2) + core)

    in_pair, out_pair = 1 + 2 * zl, 3 - 2 * zl
    along = (0, 3, 1, 2)

    def b_slot(i):
        if i == 0:
            return bc(0, 0, 0, 0, 4, 1, 0)
        if i == 1:
            return bc(1, 0, 0, 0, 4, 3, 0)
        if i == 2:
            return bc(2, 0, 0, 0, 4, 2, 0)
        if i == 3:
            return bc(3, 2, 0, 0, 4, 0, 2)
        dp = along[(i - 4) % 4]
        if i < 8:
            return bc(i, dp, 0, 0, 4, 0, 1)
        if i < 12:
            return bc(i, dp, 0, 0, 4, 0, 3)
        if i < 15:
            return bc(i, dp, jnp.where(first, 3, in_pair), 0, 2, 0, jnp.where(first, 1, out_pair))
        return bc(i, dp, jnp.where(first, 1, in_pair), 2, 2, 0, jnp.where(first, 3, out_pair))

    b_used = [i for i in range(19) if i != 15]

    def b_core(dp, dq):
        ref = bref(dp, dq, 0, 4)
        i = dp * 4 + dq - 1
        return copy(ref, ref, bc_s.at[i], bc_r.at[i], r, cs)

    def b_start(*slots):
        for i in slots:
            b_slot(i).start()

    def b_wait(*slots):
        for i in slots:
            b_slot(i).wait_recv()

    def b_swap(*pairs):
        for p in pairs:
            b_core(*p).start()

    livr[r] = (present[...] * valid[pl.ds(r, 1), :]).astype(F32)
    loads[0].wait()
    ft[zl] = fam[pl.ds(4 * zl, 4)]
    pl.semaphore_wait(barrier, jnp.where(target == c, 51, 53))
    for g in range(G):
        zc(g).start()
    for g in range(G):
        for s in (2 * g, 2 * g + 1):
            nall[x, zl, s] = norm(ft[zl, s].astype(F32)).astype(BF)
        for i in (0, 1):
            nc(g, i).start()

    def lv(k):
        return copy(livr.at[r], livr.at[r], lv_s.at[k], lv_r.at[k], wrap(r + k, NR), c)

    for k in range(1, NR):
        lv(k).start()

    def bias_step(t, carry):
        lo = pair[pl.ds(t * 8, 8)]
        hi = pair[pl.ds(64 + t * 8, 8)]
        both = jnp.concatenate([lo, hi], axis=1).reshape(1024, 128)
        off = both.astype(F32) - dot(both, jnp.full((128, 128), 1 / 128, BF))
        rows = (off * lax.rsqrt(jnp.mean(off * off, axis=-1, keepdims=True) + EPS)).astype(BF)
        b = dot_t(wb[...], rows)
        for i in range(8):
            bscr[pl.ds(t * 64 + i * 8, 8), :] = b[:, i * 128:(i + 1) * 128]
        return carry

    loads[1].wait()
    lax.fori_loop(0, 8, bias_step, 0, unroll=8)
    for h in range(H):
        mine[h] = bscr[pl.ds(h, 64, stride=8), :].astype(BF)
    sib_copy = copy(mine, sib, sb_s, sb_r, r, cs)
    sib_copy.start()

    def pass_on(g, i):
        for k in (i, i + 1):
            nc(g, k).wait_recv()
        for k in (i + 4, i + 5):
            nc(g, k).start()

    def partner(g):
        zc(g).wait_recv()
        for s in (2 * g, 2 * g + 1):
            nall[x, 1 - zl, s] = norm(ft[1 - zl, s].astype(F32)).astype(BF)
        for i in (2, 3):
            nc(g, i).start()

    def query(zb, s):
        rows = nall[x, zb, s]
        qs[s, pl.ds(pl.multiple_of(zb * R, R), R), :] = (dot(rows, wh[0]) * (HD ** -0.5)).astype(BF)
        gs[s, pl.ds(pl.multiple_of(zb * R, R), R), :] = sigmoid(dot(rows, wh[3]))

    sib_copy.wait_recv()
    low = lax.broadcasted_iota(jnp.int32, (64, 128), 1) < 64
    for h in range(H):
        a = mine[h].astype(F32)
        b = sib[h].astype(F32)
        left_part = jnp.where(first, a, b)
        right_part = jnp.where(first, b, a)
        ball[zl, blk, h, 0:64, :] = jnp.where(low, left_part, pltpu.roll(right_part, 64, 1)).astype(BF)
        ball[zl, blk, h, 64:128, :] = jnp.where(low, pltpu.roll(left_part, 64, 1), right_part).astype(BF)
    b_start(0, 1, 2, 4, 8)
    partner(0)
    partner(1)
    loads[2].wait()
    query(zl, 0)
    pass_on(0, 0)
    b_wait(0, 1)
    b_start(5, 9, 6, 10)
    b_swap((3, 0), (1, 0))
    b_wait(2)
    b_start(7, 11, 3)
    b_swap((2, 0))
    query(zl, 1)
    b_wait(4, 8)
    b_start(12, 16)
    b_swap((0, 3), (0, 1))
    pass_on(0, 2)
    query(zl, 2)
    pass_on(1, 0)
    query(zl, 3)
    b_wait(5, 9)
    b_start(13, 17)
    b_swap((3, 3), (3, 1))
    query(1 - zl, 0)
    b_wait(6, 10)
    b_start(14, 18)
    b_swap((1, 3), (1, 1))
    pass_on(1, 2)

    for k in range(1, NR):
        lv(k).wait_recv()
    lres[c] = livr[r]
    lcol[c] = livr[blk]

    def lr(k):
        return copy(livr.at[r], lres.at[c], lr_s.at[k], lr_r.at[k], r, wrap(c + k, NC))

    def lc(k):
        to = wrap(c + k, NC)
        return copy(livr.at[to // 2], lcol.at[c], lc_s.at[k], lc_r.at[k], r, to)

    for k in range(1, NC):
        lr(k).start()
        lc(k).start()

    for s in (1, 2, 3):
        query(1 - zl, s)
    b_wait(12, 16)
    b_swap((0, 2))
    b_wait(7, 11)
    b_swap((2, 3), (2, 1))

    def keys_values(g):
        for i in (4, 5, 6, 7):
            nc(g, i).wait_recv()
        for s in (2 * g, 2 * g + 1):
            for b in range(NR):
                rows = nall[b // 2, b % 2, s]
                ks[s, b * R:(b + 1) * R, :] = dot(rows, wh[1]).astype(BF)
                vs[s, b * R:(b + 1) * R, :] = dot(rows, wh[2]).astype(BF)

    keys_values(0)
    b_wait(13, 17)
    b_swap((3, 2))
    b_wait(14, 18)
    b_swap((1, 2))
    b_wait(3)
    b_swap((2, 2))
    loads[3].wait()
    for i in range(1, 16):
        b_core(i // 4, i % 4).wait_recv()

    def mc(g, zb, k):
        to = wrap(c + k, NC)
        return copy(
            snd.at[zb, to, pl.ds(g * 16, 16)], rcv.at[c, zl, pl.ds(g * 16, 16)],
            m_s.at[g, jnp.where(zb == zl, 0, 1), k], m_r.at[g, jnp.where(zb == zl, 0, 1), k],
            2 * x + zb, to,
        )

    def group(g):
        def row_one(i, carry):
            s = 2 * g + i
            keep = jnp.concatenate([livr[b, pl.ds(4 * zl + s, 1), :] for b in range(NR)], axis=1) > 0.5

            def score(h, raw):
                bias = jnp.concatenate(
                    [jnp.concatenate([ball[zb, b, h] for b in range(NR)], axis=1) for zb in range(2)], axis=0
                )
                return jnp.where(keep, raw + bias.astype(F32), -MASK_BIG)

            o = attend(qs[s], ks[s], vs[s], score, 1)
            delta = dot((gs[s] * o).astype(BF), wo[...])
            for zb in range(2):
                midf[i, zb] = ft[zb, s].astype(F32) + delta[zb * R:(zb + 1) * R]
            return carry

        lax.fori_loop(0, 2, row_one, 0)
        for zb in range(2):
            for t in range(NC):
                two = jnp.concatenate([midf[i, zb, t * 8:(t + 1) * 8, :] for i in range(2)], axis=0)
                snd[zb, t, g * 16:(g + 1) * 16, :] = two.astype(BF)
        for k in range(NC):
            mc(g, 1 - zl, k).start()
            if k > 0:
                mc(g, zl, k).start()

    group(0)
    keys_values(1)
    group(1)
    rcv[c, zl] = snd[zl, c]

    for k in range(1, NC):
        lr(k).wait_recv()
        lc(k).wait_recv()
    by_res = lres[...].reshape(R, R).T
    cmask[...] = by_res
    ltt[...] = lcol[...].reshape(R, R).T
    right_live = ltt[pl.ds(pl.multiple_of(core * 64, 64), 64), :]
    inv[...] = 1.0 / jnp.maximum(dot_t(right_live.astype(BF), by_res.astype(BF)), 1.0)
    for i in (4, 5, 6):
        loads[i].wait()
    wzt[...] = wz[...].astype(F32).T.astype(BF)
    for g in range(G):
        for k in range(NC):
            mc(g, 1 - zl, k).wait_recv()
            if k > 0:
                mc(g, zl, k).wait_recv()
        for t in range(0, NC, 4):
            mid = rcv[t:t + 4, :, g * 16:(g + 1) * 16, :].reshape(128, D).astype(F32)
            normed = norm(mid)
            for u in range(8):
                to = slice(t * 64 + u * 32 + g * 16, t * 64 + u * 32 + g * 16 + 16)
                for i in range(2):
                    xf[i, to, :] = mid[u * 16:(u + 1) * 16, i * 128:(i + 1) * 128]
                    nf[i, to, :] = normed[u * 16:(u + 1) * 16, i * 128:(i + 1) * 128]

    def rows_of(ref, p):
        return jnp.concatenate(
            [
                jnp.concatenate([ref[i, pl.ds(p * NB + b, R, stride=8), :] for i in range(2)], axis=1)
                for b in range(NB)
            ],
            axis=0,
        )

    def col_half(p):
        rows = rows_of(nf, p).astype(BF)
        cqs[...] = (dot(rows, wv[0]) * (HD ** -0.5)).astype(BF)
        cks[...] = dot(rows, wv[1]).astype(BF)
        cvs[...] = dot(rows, wv[2]).astype(BF)
        cgs[...] = sigmoid(dot(rows, wv[3]))
        for b in range(NB):
            row = cmask[pl.ds(c * 8 + p * NB + b, 1), :]
            span = slice(b * R, (b + 1) * R)

            def score(h, raw):
                return jnp.where(row > 0.5, raw, -MASK_BIG)

            o = attend(cqs[span, :], cks[span, :], cvs[span, :], score, 2)
            cos[span, :] = (cgs[span, :] * o).astype(BF)
        up = (rows_of(xf, p) + dot(cos[...], wvo[...])).astype(BF).astype(F32)
        both = dot_t(wlr[...], norm(up).astype(BF))
        for b in range(NB):
            span = slice(b * R, (b + 1) * R)
            for i in range(2):
                upf[i, pl.ds(p * NB + b, R, stride=8), :] = up[span, i * 128:(i + 1) * 128]
            one = both[:, span] * cmask[pl.ds(c * 8 + p * NB + b, 1), :]
            lf[pl.ds(p * 128 + b, HD, stride=NB), :] = one[:HD]
            rf[(p * NB + b) * HD:(p * NB + b + 1) * HD, :] = one[HD:]
        lrcv[c, p * 128:(p + 1) * 128, :] = lf[p * 128:(p + 1) * 128, :].astype(BF)
        rsnd[p * 128:(p + 1) * 128, :] = rf[p * 128:(p + 1) * 128, :].astype(BF)

    def lslot(p, k):
        ref = lrcv.at[c, pl.ds(p * 128, 128)]
        return copy(ref, ref, le_s.at[p, k], le_r.at[p, k], r, wrap(c + 2 * k, NC))

    def lswap(p, k):
        ref = lrcv.at[wrap(c - 2 * k, NC), pl.ds(p * 128, 128)]
        return copy(ref, ref, lw_s.at[p, k], lw_r.at[p, k], r, cs)

    near_first = (2, 6, 4, 1, 7, 3, 5)

    place = lax.rem(c, 8)

    def rcopy(p, k):
        span = pl.ds(p * 128, 128)
        return copy(rsnd.at[span], rrcv.at[place, span], ri_s.at[p, k], ri_r.at[p, place], k, target)

    def left_send(p):
        for k in near_first:
            lslot(p, k).start()
        lswap(p, 0).start()

    def left_swap(p):
        for k in near_first:
            lslot(p, k).wait_recv()
            lswap(p, k).start()

    def right_send(p):
        for k in range(8):
            @pl.when(self_row != k)
            def _():
                rcopy(p, k).start()

    def right_wait(p):
        span = pl.ds(p * 128, 128)
        for k in range(8):
            @pl.when(jnp.logical_or(blk != r, 8 * core + k != c))
            def _():
                copy(rsnd.at[span], rrcv.at[k, span], ri_s.at[p, k], ri_r.at[p, k], r, c).wait_recv()

    col_half(0)
    left_send(0)
    right_send(0)
    col_half(1)
    left_send(1)

    @pl.when(target == c)
    def _():
        rrcv[place] = rsnd[...]

    def uc(k):
        to = wrap(c + k, NC)
        return copy(back_snd.at[to], back_rcv.at[c], u_s.at[k], u_r.at[k], r, to)

    left_swap(0)
    right_send(1)

    for i in range(2):
        back_snd[:, :, i * 128:(i + 1) * 128] = upf[i].reshape(NC, 64, 128).astype(BF)

    sib_copy.wait_send()
    for g in range(G):
        zc(g).wait_send()
    for g in range(G):
        for i in range(8):
            nc(g, i).wait_send()
        for k in range(NC):
            mc(g, 1 - zl, k).wait_send()
            if k > 0:
                mc(g, zl, k).wait_send()
    for k in range(1, NR):
        lv(k).wait_send()
    for k in range(1, NC):
        lr(k).wait_send()
        lc(k).wait_send()
    for i in b_used:
        b_slot(i).wait_send()
    for i in range(1, 16):
        b_core(i // 4, i % 4).wait_send()

    left_swap(1)
    for k in range(1, NC):
        uc(k).start()
    back_rcv[c] = back_snd[c]
    for p in range(2):
        for i in range(8):
            lswap(p, i).wait_recv()
    low4 = lax.rem(lax.broadcasted_iota(jnp.int32, (R, 128), 0), 8) < 4
    for m in range(16):
        a = lrcv[:, m * 8:(m + 1) * 8, :].astype(F32).reshape(R, 128)
        b = lrcv[:, 128 + m * 8:128 + (m + 1) * 8, :].astype(F32).reshape(R, 128)
        ltall[2 * m * R:(2 * m + 1) * R, :] = jnp.where(low4, a, pltpu.roll(b, 4, 0)).astype(BF)
        ltall[(2 * m + 1) * R:(2 * m + 2) * R, :] = jnp.where(low4, pltpu.roll(a, R - 4, 0), b).astype(BF)

    def out_copy(q):
        return pltpu.make_async_copy(blocks.at[q], pair_out.at[:, pl.ds(q * 16, 16), :], o_s.at[q])

    def sixteen(q, p):
        rows = jnp.concatenate([rrcv[4 * q + t, p * 128:(p + 1) * 128, :] for t in range(4)], axis=0)
        o = dot_t(rows, ltall[...]).astype(BF)
        for j0 in range(0, 16, 2):
            two = jnp.concatenate(
                [
                    jnp.concatenate([o[j * HD:(j + 1) * HD, i * R:(i + 1) * R] for i in range(HD)], axis=0)
                    for j in (j0, j0 + 1)
                ],
                axis=1,
            )
            prod = dot(wzt[...], two)
            for i in range(2):
                j = q * 32 + (j0 + i) // NB * 8 + p * NB + (j0 + i) % NB
                one = prod[:, i * R:(i + 1) * R] * inv[pl.ds(j, 1), :]
                acc[pl.ds(j, R, stride=64), :] = one.T

    def first_half(q, carry):
        sixteen(q, 0)
        return carry

    right_wait(0)
    lax.fori_loop(0, 2, first_half, 0, unroll=2)
    right_wait(1)
    for q in range(2):
        sixteen(q, 1)
        for t in (2 * q, 2 * q + 1):
            blocks[t] = acc[...].reshape(R, 64, 128)[:, t * 16:(t + 1) * 16, :].astype(BF)
            out_copy(t).start()
    for k in range(1, NC):
        uc(k).wait_recv()
    for s in range(S):
        align[s] = jnp.concatenate([back_rcv[t, s * 8:(s + 1) * 8, :] for t in range(NC)], axis=0)
    for q in range(4):
        out_copy(q).wait()

    for k in range(1, NC):
        uc(k).wait_send()
    for p in range(2):
        for k in near_first:
            lslot(p, k).wait_send()
        for i in range(8):
            lswap(p, i).wait_send()
        for k in range(8):
            @pl.when(self_row != k)
            def _():
                rcopy(p, k).wait_send()


def relay_kernel(a, b, a_out, b_out, a_mid, b_mid, sem):
    refs = [(a, a_mid, a_out, pl.ds(0, S))]
    refs += [(b, b_mid, b_out, pl.ds(i * 32, 32)) for i in range(4)]
    into = [pltpu.make_async_copy(p.at[rows], q.at[rows], sem.at[0, i]) for i, (p, q, _, rows) in enumerate(refs)]
    back = [pltpu.make_async_copy(q.at[rows], o.at[rows], sem.at[1, i]) for i, (_, q, o, rows) in enumerate(refs)]
    for cp in into:
        cp.start()
    for one, two in zip(into, back):
        one.wait()
        two.start()
    for cp in back:
        cp.wait()


def per_device(fam, pair, present, valid, wh, wo, wb, wv, wvo, wlr, wz):
    vm = pl.BlockSpec(memory_space=pltpu.VMEM)
    anywhere = pl.BlockSpec(memory_space=pl.ANY)
    dma = pltpu.SemaphoreType.DMA

    def sems(*shape):
        return [dma(shape), dma(shape)]

    scratch = [
        pltpu.VMEM((S, R, D), BF),
        pltpu.VMEM((R, 64, 128), BF),
        pltpu.VMEM((4, D, D), BF),
        pltpu.VMEM((D, D), BF),
        pltpu.VMEM((4, D, D), BF),
        pltpu.VMEM((D, D), BF),
        pltpu.VMEM((1024, 128), BF),
        pltpu.VMEM((2, 4, R, D), BF),
        pltpu.VMEM((4, 2, 4, R, D), BF),
        pltpu.VMEM((NR, S, R), F32),
        pltpu.VMEM((NC, S, R), F32),
        pltpu.VMEM((NC, S, R), F32),
        pltpu.VMEM((512, 128), F32),
        pltpu.VMEM((H, 64, 128), BF),
        pltpu.VMEM((H, 64, 128), BF),
        pltpu.VMEM((2, NR, H, R, 128), BF),
        pltpu.VMEM((4, 2 * R, D), BF),
        pltpu.VMEM((4, 2 * R, D), F32),
        pltpu.VMEM((4, NR * R, D), BF),
        pltpu.VMEM((4, NR * R, D), BF),
        pltpu.VMEM((2, 2, R, D), F32),
        pltpu.VMEM((NB * R, D), BF),
        pltpu.VMEM((NB * R, D), BF),
        pltpu.VMEM((NB * R, D), BF),
        pltpu.VMEM((NB * R, D), F32),
        pltpu.VMEM((NB * R, D), BF),
        pltpu.VMEM((2, NC, 32, D), BF),
        pltpu.VMEM((NC, 2, 32, D), BF),
        pltpu.VMEM((2, 1024, 128), F32),
        pltpu.VMEM((2, 1024, 128), F32),
        pltpu.VMEM((2, 1024, 128), F32),
        pltpu.VMEM((NC, 64, D), BF),
        pltpu.VMEM((NC, 64, D), BF),
        pltpu.VMEM((256, 128), F32),
        pltpu.VMEM((256, 128), F32),
        pltpu.VMEM((NC, 256, 128), BF),
        pltpu.VMEM((256, 128), BF),
        pltpu.VMEM((8, 256, 128), BF),
        pltpu.VMEM((R, 128), F32),
        pltpu.VMEM((R, 128), F32),
        pltpu.VMEM((64, 128), F32),
        pltpu.VMEM((HD * R, 128), BF),
        pltpu.VMEM((128, 1024), BF),
        pltpu.VMEM((R * 64, 128), F32),
        pltpu.VMEM((4, R, 16, 128), BF),
        *sems(G), *sems(G, 8), *sems(8), *sems(16), *sems(16), dma, dma, *sems(20), *sems(15),
        *sems(G, 2, 16), *sems(16), *sems(2, 8), *sems(2, 8), *sems(2, 8), dma((4,)), dma((7,)),
    ]
    align, pair_out = pl.pallas_call(
        msa_kernel,
        out_shape=(jax.ShapeDtypeStruct((S, R, D), BF), jax.ShapeDtypeStruct((R, 64, 128), BF)),
        in_specs=[anywhere, anywhere, vm, vm, anywhere, anywhere, vm, anywhere, anywhere, vm, anywhere],
        out_specs=(vm, pl.BlockSpec(memory_space=pl.ANY)),
        scratch_shapes=scratch,
        compiler_params=pltpu.CompilerParams(
            has_side_effects=True, collective_id=0, vmem_limit_bytes=60 * 1024 * 1024
        ),
        name="msa",
    )(
        fam, pair, present, valid.reshape(NR, R), wh, wo, wb.T, wv, wvo,
        wlr.transpose(0, 2, 1).reshape(64, D), wz,
    )
    return pl.pallas_call(
        relay_kernel,
        out_shape=(jax.ShapeDtypeStruct((S, R, D), BF), jax.ShapeDtypeStruct((R, 64, 128), BF)),
        in_specs=[anywhere] * 2,
        out_specs=(anywhere,) * 2,
        scratch_shapes=[pltpu.VMEM((S, R, D), BF), pltpu.VMEM((R, 64, 128), BF), dma((2, 5))],
        compiler_params=pltpu.CompilerParams(vmem_limit_bytes=60 * 1024 * 1024),
        name="relay",
    )(align, pair_out)


def solution(mesh):
    in_specs = (P("col", "row", None), P("row", "col", None), P("col", "row")) + (P(),) * 8
    out_specs = (P("col", "row", None), P("row", "col", None))
    return jax.shard_map(per_device, mesh=mesh, in_specs=in_specs, out_specs=out_specs, check_vma=False)
```
